128 devices in a mesh: fsdp: 32 (over y, x, core), tp: 4 (over z).
Axes of the slice: x: 4, y: 4, z: 4, core: 2. Of those that a mesh axis runs over, the one named last changes fastest.
Arguments:
- weight: float32 [4096, 16384], P('fsdp', 'tp'), may hold values from -0.75 to 0.75
- momentum: float32 [4096, 16384], P('fsdp', 'tp'), may hold values from -6 to 6
- gradient: bfloat16 [4096, 16384], P('fsdp', 'tp'), may hold values from -6 to 6
- factor: float32 [16384, 256], P('tp'), may hold values from -0.046875 to 0.046875
- decay: float32 [], replicated, may hold values from 0.8 to 0.98
- rate: float32 [], replicated, may hold values from 0.01 to 0.1
Outputs:
- new_weight: float32 [4096, 16384], P('fsdp', 'tp')
- new_momentum: float32 [4096, 16384], P('fsdp', 'tp')
- new_factor: float32 [16384, 256], P('tp')
The draws below stay inside these ranges and needn't reach their ends.
All inputs are finite; a program needn't handle non-finite values.
Results may differ from the reference program's by a relative error of at most 0.0003.
Values sent between devices are 32-bit elements; how exact they have to be, the bound alone decides.
A program may use at most 64 MiB of HBM per device.

```python
import math
import jax
import jax.numpy as jnp
from jax import lax

COLS = 16384
RANK = 256
ROWS = 4096


def level_of(rng, shape, shards, low, high):
    def one(position, shards_of):
        draws = jax.random.uniform(jax.random.fold_in(jax.random.fold_in(rng, 6), position), (shards_of,), jnp.float32, low / len(shards), high / len(shards))
        return jnp.repeat(jnp.exp(draws), shape[position] // shards_of).reshape((-1,) + (1,) * (len(shape) - position - 1))

    factor_of = one(*shards[0])
    for cut in shards[1:]:
        factor_of = factor_of * one(*cut)
    return factor_of


def scatter_about(own_key, shape, width, most, shards=(), dtype=jnp.bfloat16):
    gain = level_of(own_key, shape, shards, -0.22, 0.18) if shards else 1.0
    entries = jax.random.normal(own_key, shape, jnp.float32) * width * gain
    return jnp.minimum(jnp.maximum(entries, -most), most).astype(dtype)


def setup_inputs(seed: int = 0) -> dict:
    streams_of = jax.random.split(jax.random.key(seed), 7)
    return {
        "weight": scatter_about(streams_of[0], (ROWS, COLS), 0.05, 0.75, ((0, 32), (1, 4)), jnp.float32),
        "momentum": scatter_about(streams_of[1], (ROWS, COLS), 1.0, 6.0, ((0, 32), (1, 4)), jnp.float32),
        "gradient": scatter_about(streams_of[2], (ROWS, COLS), 1.0, 6.0, ((0, 32), (1, 4))),
        "factor": scatter_about(streams_of[3], (COLS, RANK), COLS ** -0.5, 0.046875, ((0, 4),), jnp.float32),
        "decay": jnp.clip(jax.random.uniform(streams_of[4], (), jnp.float32, 0.8, 0.98), 0.8, 0.98),
        "rate": jnp.clip(jnp.exp(jax.random.uniform(streams_of[5], (), jnp.float32, math.log(0.01), math.log(0.1))), 0.01, 0.1),
    }


def reference(weight, momentum, gradient, factor, decay, rate):
    high = lax.Precision.HIGHEST
    buffer = momentum + gradient.astype(jnp.float32)
    left = jnp.dot(buffer.astype(jnp.float32), factor.astype(jnp.float32), precision=high, preferred_element_type=jnp.float32)
    gram = jnp.dot(left.T.astype(jnp.float32), left.astype(jnp.float32), precision=high, preferred_element_type=jnp.float32)
    lower = jnp.linalg.cholesky(gram)
    basis = lax.linalg.triangular_solve(lower, left, left_side=False, lower=True, transpose_a=True)
    right = jnp.dot(buffer.T.astype(jnp.float32), basis.astype(jnp.float32), precision=high, preferred_element_type=jnp.float32)
    new_momentum = buffer - (1.0 - decay) * jnp.dot(basis.astype(jnp.float32), right.T.astype(jnp.float32), precision=high, preferred_element_type=jnp.float32)
    squares = lax.optimization_barrier(jnp.sum(right * right, axis=0))
    new_factor = right * lax.rsqrt(squares + 1e-06)
    scale = rate * jnp.sqrt(jnp.float32(ROWS * COLS / RANK))
    new_weight = weight - scale * jnp.dot(basis.astype(jnp.float32), new_factor.T.astype(jnp.float32), precision=high, preferred_element_type=jnp.float32)
    return (new_weight, new_momentum, new_factor)
```

```python
import jax
import jax.numpy as jnp
from jax import lax
from jax.experimental import pallas as pl
from jax.experimental.pallas import tpu as pltpu
from jax.sharding import PartitionSpec as P

F32 = jnp.float32
BF16 = jnp.bfloat16
HIGH = lax.Precision.HIGHEST
MESH = pl.DeviceIdType.MESH
NX = NY = NZ = 4
ROWS, COLS, RANK = 128, 4096, 256
HALF = COLS // 2
QUARTER = HALF // 2
BIG = QUARTER // 4
SMALL = BIG // 4
PLANE = [(dx, dy, dc) for dx in range(NX) for dy in range(NY) for dc in range(2) if dx or dy or dc]
CHIPS = [(dx, dy) for dx in range(NX) for dy in range(NY) if dx or dy]
RING = (1, 3, 2)


def split(x):
    hi = x.astype(BF16)
    return hi, (x - hi.astype(F32)).astype(BF16)


def dot3(a, b, dims):
    (ah, al), (bh, bl) = a, b

    def one(p, q):
        return lax.dot_general(p, q, (dims, ((), ())), preferred_element_type=F32)

    return one(ah, bh) + (one(ah, bl) + one(al, bh))


def dot6(a, b, dims):
    return lax.dot_general(a, b, (dims, ((), ())), precision=HIGH, preferred_element_type=F32)


def row_of(t, s):
    return jnp.broadcast_to(t[s : s + 1, :], (8, 128))


def lane_of(t, l):
    return jnp.broadcast_to(t[:, l : l + 1], (8, 128))


def eliminate(d):
    nb, nt = 64, 8
    lane = lax.broadcasted_iota(jnp.int32, (8, 128), 1)
    sub = lax.broadcasted_iota(jnp.int32, (8, 128), 0)
    w = []
    for i in range(nt):
        tile = jnp.concatenate([d[8 * i : 8 * i + 8, :], jnp.zeros((8, 128 - nb), F32)], axis=1)
        w.append(jnp.where(lane == nb + 8 * i + sub, 1.0, tile))
    out = []
    for k in range(nt):
        tile = w[k]
        cs = [lane_of(tile, 8 * k + j) for j in range(8)]
        others = [[lane_of(w[i], 8 * k + j) for j in range(8)] for i in range(k + 1, nt)]
        v = tile
        for p in range(8):
            piv = row_of(cs[p], p)
            inv = 1.0 / piv
            row = row_of(tile, p)
            mine = sub == p
            v = jnp.where(mine, row * lax.rsqrt(piv), v)
            rn = row * inv
            cz = jnp.where(mine, 0.0, cs[p])
            tile = jnp.where(mine, rn, tile) - cz * rn
            for j in range(p + 1, 8):
                rj = row_of(cs[j], p) * inv
                cs[j] = jnp.where(mine, rj, cs[j]) - cz * rj
        out.append(v)
        if k + 1 < nt:
            ts = [row_of(tile, p) for p in range(8)]
            for i in range(k + 1, nt):
                acc = [others[i - k - 1][p] * ts[p] for p in range(8)]
                while len(acc) > 1:
                    acc = [acc[q] + acc[q + 1] for q in range(0, len(acc), 2)]
                w[i] = w[i] - acc[0]
    return jnp.concatenate([o[:, nb : 2 * nb] for o in out], axis=0)


def factor_block(m, k):
    lo, hi = 64 * k, 64 * k + 64
    v = dot6(eliminate(m[lo:hi, lo:hi]), m[lo:hi, :], ((1,), (0,)))
    m[lo:hi, :] = v
    if hi < RANK:
        ut = v[:, :RANK].T[hi:, :]
        m[hi:, :] -= dot6(ut, v, ((1,), (0,)))


def reduce_kernel(
    mom_hbm, grad_hbm, fac_hbm, right_hbm, basis_out, norm_out,
    mom, grad, fac, peer_b, zbuf, left, gsend, grecv, gown, gram, m, gp,
    rs1, rs2, right, sq_own, sq_in, sq_z, sq_zin,
    load_sem, b_sem, z_sem, l_sem, g_sem, gg_sem, rs1_sem, rs2_sem, ag1_sem, ag2_sem, core_sem, sq_sem, sqz_sem, out_sem,
):
    f = lax.axis_index("fsdp")
    z = lax.axis_index("tp")
    y, x, c = f // 8, (f // 2) % 4, f % 2

    def at(dx=0, dy=0, dc=0, dz=0):
        return ((((y + dy) % 4) * 4 + (x + dx) % 4) * 2 + (c + dc) % 2, (z + dz) % 4)

    def send(src, dst, sems, where):
        cp = pltpu.make_async_remote_copy(
            src, dst, sems.at[0], sems.at[1], device_id=where, device_id_type=MESH
        )
        cp.start()
        return cp

    def rows(start, size):
        return pl.ds(pl.multiple_of(start, size), size)

    loads = []
    for q in range(4):
        cols = pl.ds(q * 1024, 1024)
        trio = [
            pltpu.make_async_copy(mom_hbm.at[:, cols], mom.at[:, cols], load_sem.at[q, 0]),
            pltpu.make_async_copy(grad_hbm.at[:, cols], grad.at[:, cols], load_sem.at[q, 1]),
            pltpu.make_async_copy(fac_hbm.at[cols, :], fac.at[cols, :], load_sem.at[q, 2]),
        ]
        for cp in trio:
            cp.start()
        loads.append(trio)

    barrier = pltpu.get_barrier_semaphore()
    for dx, dy, dc in PLANE:
        pl.semaphore_signal(barrier, inc=1, device_id=at(dx, dy, dc), device_id_type=MESH)
    for dz in RING:
        pl.semaphore_signal(barrier, inc=1, device_id=at(dz=dz), device_id_type=MESH)

    part = None
    for q in range(4):
        for cp in loads[q]:
            cp.wait()
        cols = pl.ds(q * 1024, 1024)
        mom[:, cols] = mom[:, cols] + grad[:, cols].astype(F32)
        p = dot6(mom[:, cols], fac[cols, :], ((1,), (0,)))
        part = p if part is None else part + p
    zbuf[z] = part
    pl.semaphore_wait(barrier, len(PLANE) + len(RING))
    z_cps = [send(zbuf.at[z], zbuf.at[z], z_sem.at[i], at(dz=dz)) for i, dz in enumerate(RING)]
    b_cp = send(mom.at[:, rows((1 - c) * HALF, HALF)], peer_b, b_sem, at(dc=1))
    for cp in z_cps:
        cp.wait_recv()
    left[0] = (zbuf[0] + zbuf[1]) + (zbuf[2] + zbuf[3])
    l_cp = send(left.at[0], left.at[1], l_sem, at(dc=1))
    l_cp.wait_recv()
    both = left[...].reshape(2 * ROWS, RANK)

    mine = left[:, :, rows(c * 128, 128)].reshape(2 * ROWS, 128)
    gsend[...] = dot6(mine, both, ((0,), (0,)))
    chip = y * 4 + x
    g_cps = []
    for i, (dx, dy) in enumerate(CHIPS):
        other = ((y + dy) % 4) * 4 + (x + dx) % 4
        g_cps.append(send(gsend.at[rows(other * 8, 8), :], grecv.at[i], g_sem.at[i], at(dx, dy)))

    b_cp.wait_recv()
    lh, ll = split(both)

    def product(start):
        own = mom[:, rows(c * HALF + start, BIG)]
        cat = jnp.concatenate([own, peer_b[:, rows(start, BIG)]], axis=0)
        gp[rows(start, BIG), :] = dot3(split(cat), (lh, ll), ((0,), (0,)))

    rs1_cps = []
    for i, d in enumerate((2, 1, 3)):
        ca, cb = ((x + d) % 4) * BIG, QUARTER + ((y + d) % 4) * BIG
        product(ca)
        rs1_cps.append(send(gp.at[rows(ca, BIG), :], rs1.at[0, i], rs1_sem.at[0, i], at(dx=d)))
        product(cb)
        rs1_cps.append(send(gp.at[rows(cb, BIG), :], rs1.at[1, i], rs1_sem.at[1, i], at(dy=d)))
    own_a, own_b = x * BIG, QUARTER + y * BIG
    product(own_a)
    product(own_b)

    total = gsend[rows(chip * 8, 8), :]
    for i, cp in enumerate(g_cps):
        cp.wait_recv()
        total = total + grecv[i]
    gown[...] = total
    gg_cps = []
    for i, (dx, dy, dc) in enumerate(PLANE):
        gg_cps.append(send(gown, gram.at[c * 16 + chip], gg_sem.at[i], at(dx, dy, dc)))
    gram[c * 16 + chip] = total
    for cp in gg_cps:
        cp.wait_recv()
    m[:, :RANK] = gram[...].reshape(RANK, RANK)
    r_id = lax.broadcasted_iota(jnp.int32, (RANK, RANK), 0)
    c_id = lax.broadcasted_iota(jnp.int32, (RANK, RANK), 1)
    m[:, RANK:] = jnp.where(r_id == c_id, 1.0, 0.0).astype(F32)
    factor_block(m, 0)
    factor_block(m, 1)

    for cp in rs1_cps:
        cp.wait_recv()
    gp[rows(own_a, BIG), :] = (gp[rows(own_a, BIG), :] + rs1[0, 0]) + (rs1[0, 1] + rs1[0, 2])
    gp[rows(own_b, BIG), :] = (gp[rows(own_b, BIG), :] + rs1[1, 0]) + (rs1[1, 1] + rs1[1, 2])
    rs2_cps = []
    for i, d in enumerate((2, 1, 3)):
        ca, cb = own_a + ((y + d) % 4) * SMALL, own_b + ((x + d) % 4) * SMALL
        rs2_cps.append(send(gp.at[rows(ca, SMALL), :], rs2.at[0, i], rs2_sem.at[0, i], at(dy=d)))
        rs2_cps.append(send(gp.at[rows(cb, SMALL), :], rs2.at[1, i], rs2_sem.at[1, i], at(dx=d)))

    factor_block(m, 2)
    factor_block(m, 3)
    inverse = m[:, RANK:]

    for cp in rs2_cps:
        cp.wait_recv()
    small_a, small_b = own_a + y * SMALL, own_b + x * SMALL
    done_a = (gp[rows(small_a, SMALL), :] + rs2[0, 0]) + (rs2[0, 1] + rs2[0, 2])
    done_b = (gp[rows(small_b, SMALL), :] + rs2[1, 0]) + (rs2[1, 1] + rs2[1, 2])
    part = dot6(jnp.concatenate([done_a, done_b], axis=0), inverse, ((1,), (1,)))
    base = c * HALF
    right[rows(base + small_a, SMALL), :] = part[:SMALL]
    right[rows(base + small_b, SMALL), :] = part[SMALL:]

    piece_a = right.at[rows(base + small_a, SMALL), :]
    piece_b = right.at[rows(base + small_b, SMALL), :]
    ag1 = []
    for i, d in enumerate((2, 1, 3)):
        ag1.append(send(piece_a, piece_a, ag1_sem.at[0, i], at(dy=d)))
        ag1.append(send(piece_b, piece_b, ag1_sem.at[1, i], at(dx=d)))
    sq_own[0:1, :] = jnp.sum(part * part, axis=0, keepdims=True)
    sq_cps = []
    for i, (dx, dy, dc) in enumerate(PLANE):
        sq_cps.append(send(sq_own.at[0:1], sq_in.at[i, 0:1], sq_sem.at[i], at(dx, dy, dc)))
    basis = dot6(left[0], inverse, ((1,), (1,)))
    basis_out[...] = basis
    for cp in ag1:
        cp.wait_recv()
    big_a = right.at[rows(base + own_a, BIG), :]
    big_b = right.at[rows(base + own_b, BIG), :]
    ag2 = []
    for i, d in enumerate((2, 1, 3)):
        ag2.append((send(big_a, big_a, ag2_sem.at[0, i], at(dx=d)), ((x - d) % 4) * BIG))
        ag2.append((send(big_b, big_b, ag2_sem.at[1, i], at(dy=d)), QUARTER + ((y - d) % 4) * BIG))

    starts = [own_a, own_b] + [start for _, start in ag2]
    core_cps, out_cps = {}, []

    def write(place, sem):
        cp = pltpu.make_async_copy(right.at[place, :], right_hbm.at[place, :], sem)
        cp.start()
        out_cps.append(cp)

    def arrived(k):
        place = rows(base + starts[k], BIG)
        core_cps[k] = send(right.at[place, :], right.at[place, :], core_sem.at[k], at(dc=1))
        write(place, out_sem.at[0, k])

    def taken(k):
        core_cps[k].wait_recv()
        write(rows((1 - c) * HALF + starts[k], BIG), out_sem.at[1, k])

    arrived(0)
    arrived(1)

    for cp in sq_cps:
        cp.wait_recv()
    total = sq_own[0:1, :]
    for i in range(len(PLANE)):
        total = total + sq_in[i, 0:1, :]
    sq_z[0:1, :] = total
    sqz_cps = [send(sq_z.at[0:1], sq_zin.at[i, 0:1], sqz_sem.at[i], at(dz=dz)) for i, dz in enumerate(RING)]

    order = [2 * i + h for i in (1, 2, 0) for h in (0, 1)]
    for k in order:
        ag2[k][0].wait_recv()
        arrived(2 + k)
    for cp in sqz_cps:
        cp.wait_recv()
    for i in range(len(RING)):
        total = total + sq_zin[i, 0:1, :]
    norm_out[...] = jnp.broadcast_to(lax.rsqrt(total + 1e-06), (8, RANK))
    for k in [0, 1] + [2 + k for k in order]:
        taken(k)

    for cp in z_cps + [b_cp, l_cp] + g_cps + gg_cps + rs1_cps + rs2_cps + ag1 + sq_cps + sqz_cps:
        cp.wait_send()
    for cp, _ in ag2:
        cp.wait_send()
    for cp in core_cps.values():
        cp.wait_send()
    for cp in out_cps:
        cp.wait()


def reduce_call(mom, grad, fac):
    vmem = pltpu.VMEM
    dma = pltpu.SemaphoreType.DMA
    return pl.pallas_call(
        reduce_kernel,
        out_shape=(
            jax.ShapeDtypeStruct((COLS, RANK), F32),
            jax.ShapeDtypeStruct((ROWS, RANK), F32),
            jax.ShapeDtypeStruct((8, RANK), F32),
        ),
        in_specs=[pl.BlockSpec(memory_space=pl.ANY)] * 3,
        out_specs=(
            pl.BlockSpec(memory_space=pl.ANY),
            pl.BlockSpec(memory_space=vmem),
            pl.BlockSpec(memory_space=vmem),
        ),
        scratch_shapes=[
            vmem((ROWS, COLS), F32),
            vmem((ROWS, COLS), BF16),
            vmem((COLS, RANK), F32),
            vmem((ROWS, HALF), F32),
            vmem((NZ, ROWS, RANK), F32),
            vmem((2, ROWS, RANK), F32),
            vmem((128, RANK), F32),
            vmem((len(CHIPS), 8, RANK), F32),
            vmem((8, RANK), F32),
            vmem((32, 8, RANK), F32),
            vmem((RANK, 2 * RANK), F32),
            vmem((HALF, RANK), F32),
            vmem((2, 3, BIG, RANK), F32),
            vmem((2, 3, SMALL, RANK), F32),
            vmem((COLS, RANK), F32),
            vmem((8, RANK), F32),
            vmem((len(PLANE), 8, RANK), F32),
            vmem((8, RANK), F32),
            vmem((3, 8, RANK), F32),
            dma((4, 3)),
            dma((2,)),
            dma((3, 2)),
            dma((2,)),
            dma((len(CHIPS), 2)),
            dma((len(PLANE), 2)),
            dma((2, 3, 2)),
            dma((2, 3, 2)),
            dma((2, 3, 2)),
            dma((2, 3, 2)),
            dma((8, 2)),
            dma((len(PLANE), 2)),
            dma((3, 2)),
            dma((2, 8)),
        ],
        compiler_params=pltpu.CompilerParams(
            collective_id=0, has_side_effects=True, vmem_limit_bytes=40 * 2**20
        ),
    )(mom, grad, fac)


def update_kernel(scal, w, mom, grad, right, basis, norm, new_w, new_mom, new_fac):
    decay, rate = scal[0], scal[1]
    s = norm[0:1, :]
    r = right[...]
    new_fac[...] = r * s
    q = basis[...]
    scale = rate * jnp.sqrt(jnp.float32(4096 * 16384 / RANK))
    stacked = jnp.concatenate([q * (1.0 - decay), q * (s * scale)], axis=0)
    d = dot3(split(stacked), split(r), ((1,), (1,)))
    new_mom[...] = (mom[...] + grad[...].astype(F32)) - d[:ROWS]
    new_w[...] = w[...] - d[ROWS:]


def update_call(scal, w, mom, grad, right, basis, norm):
    wide = 512
    across = pl.BlockSpec((ROWS, wide), lambda i: (0, i))
    down = pl.BlockSpec((wide, RANK), lambda i: (i, 0))
    return pl.pallas_call(
        update_kernel,
        grid=(COLS // wide,),
        out_shape=(
            jax.ShapeDtypeStruct((ROWS, COLS), F32),
            jax.ShapeDtypeStruct((ROWS, COLS), F32),
            jax.ShapeDtypeStruct((COLS, RANK), F32),
        ),
        in_specs=[
            pl.BlockSpec(memory_space=pltpu.SMEM),
            across,
            across,
            across,
            down,
            pl.BlockSpec((ROWS, RANK), lambda i: (0, 0)),
            pl.BlockSpec((8, RANK), lambda i: (0, 0)),
        ],
        out_specs=(across, across, down),
        compiler_params=pltpu.CompilerParams(vmem_limit_bytes=24 * 2**20),
    )(scal, w, mom, grad, right, basis, norm)


def body(weight, momentum, gradient, factor, decay, rate):
    right, basis, norm = reduce_call(momentum, gradient, factor)
    scal = jnp.stack([decay, rate])
    return tuple(update_call(scal, weight, momentum, gradient, right, basis, norm))


def solution(mesh):
    placed = (P("fsdp", "tp"), P("fsdp", "tp"), P("fsdp", "tp"), P("tp", None), P(), P())
    return jax.shard_map(
        body,
        mesh=mesh,
        in_specs=placed,
        out_specs=(P("fsdp", "tp"), P("fsdp", "tp"), P("tp", None)),
        check_vma=False,
    )
```

```python
import jax
import jax.numpy as jnp
from jax import lax
from jax.experimental import pallas as pl
from jax.experimental.pallas import tpu as pltpu
from jax.sharding import PartitionSpec as P

F32 = jnp.float32
BF16 = jnp.bfloat16
HIGH = lax.Precision.HIGHEST
MESH = pl.DeviceIdType.MESH
NX = NY = NZ = 4
ROWS, COLS, RANK = 128, 4096, 256
HALF = COLS // 2
QUARTER = HALF // 2
BIG = QUARTER // 4
SMALL = BIG // 4
CHIPS = [(dx, dy) for dx in range(NX) for dy in range(NY) if dx or dy]
RING = (1, 3, 2)
COLUMN = [(dz, dc) for dz in range(NZ) for dc in range(2) if dz or dc]


def split(x):
    hi = x.astype(BF16)
    return hi, (x - hi.astype(F32)).astype(BF16)


def dot3(a, b, dims):
    (ah, al), (bh, bl) = a, b

    def one(p, q):
        return lax.dot_general(p, q, (dims, ((), ())), preferred_element_type=F32)

    return one(ah, bh) + (one(ah, bl) + one(al, bh))


def dot6(a, b, dims):
    return lax.dot_general(a, b, (dims, ((), ())), precision=HIGH, preferred_element_type=F32)


def row_of(t, s):
    return jnp.broadcast_to(t[s : s + 1, :], (8, 128))


def lane_of(t, l):
    return jnp.broadcast_to(t[:, l : l + 1], (8, 128))


def eliminate(d):
    nb, nt = 64, 8
    lane = lax.broadcasted_iota(jnp.int32, (8, 128), 1)
    sub = lax.broadcasted_iota(jnp.int32, (8, 128), 0)
    w = []
    for i in range(nt):
        tile = jnp.concatenate([d[8 * i : 8 * i + 8, :], jnp.zeros((8, 128 - nb), F32)], axis=1)
        w.append(jnp.where(lane == nb + 8 * i + sub, 1.0, tile))
    out = []
    for k in range(nt):
        tile = w[k]
        cs = [lane_of(tile, 8 * k + j) for j in range(8)]
        others = [[lane_of(w[i], 8 * k + j) for j in range(8)] for i in range(k + 1, nt)]
        v = tile
        for p in range(8):
            piv = row_of(cs[p], p)
            inv = 1.0 / piv
            row = row_of(tile, p)
            mine = sub == p
            v = jnp.where(mine, row * lax.rsqrt(piv), v)
            rn = row * inv
            cz = jnp.where(mine, 0.0, cs[p])
            tile = jnp.where(mine, rn, tile) - cz * rn
            for j in range(p + 1, 8):
                rj = row_of(cs[j], p) * inv
                cs[j] = jnp.where(mine, rj, cs[j]) - cz * rj
        out.append(v)
        if k + 1 < nt:
            ts = [row_of(tile, p) for p in range(8)]
            for i in range(k + 1, nt):
                acc = [others[i - k - 1][p] * ts[p] for p in range(8)]
                while len(acc) > 1:
                    acc = [acc[q] + acc[q + 1] for q in range(0, len(acc), 2)]
                w[i] = w[i] - acc[0]
    return jnp.concatenate([o[:, nb : 2 * nb] for o in out], axis=0)


def factor_block(m, k):
    lo, hi = 64 * k, 64 * k + 64
    v = dot6(eliminate(m[lo:hi, lo:hi]), m[lo:hi, :], ((1,), (0,)))
    m[lo:hi, :] = v
    if hi < RANK:
        ut = v[:, :RANK].T[hi:, :]
        m[hi:, :] -= dot6(ut, v, ((1,), (0,)))


def reduce_kernel(
    mom_hbm, grad_hbm, fac_hbm, right_out, basis_out, norm_out,
    mom, grad, fac, peer_b, zbuf, left, gsend, grecv, gown, gram, m, gp, fwd, rs1, rs2, raw, right, basis, norm, sq_own, sq_in,
    load_sem, b_sem, z_sem, l_sem, g_sem, gg_sem, cg_sem, fwd_sem, rs1_send, rs1_sem, rs2_sem, ag1_sem, ag2_send, ag2_sem,
    core_sem, sq_sem, out_sem,
):
    f = lax.axis_index("fsdp")
    z = lax.axis_index("tp")
    y, x, c = f // 8, (f // 2) % 4, f % 2

    def at(dx=0, dy=0, dc=0, dz=0):
        return ((((y + dy) % 4) * 4 + (x + dx) % 4) * 2 + (c + dc) % 2, (z + dz) % 4)

    def copy(src, dst, send_sem, recv_sem, where):
        return pltpu.make_async_remote_copy(
            src, dst, send_sem, recv_sem, device_id=where, device_id_type=MESH
        )

    drains = []

    def send(src, dst, send_sem, recv_sem, where):
        cp = copy(src, dst, send_sem, recv_sem, where)
        cp.start()
        return cp

    def group(ref, send_sem, recv_sem):
        return copy(ref, ref, send_sem, recv_sem, at(dc=1))

    def write(src, dst, sem):
        cp = pltpu.make_async_copy(src, dst, sem)
        cp.start()
        return cp

    def rows(start, size):
        return pl.ds(pl.multiple_of(start, size), size)

    barrier = pltpu.get_barrier_semaphore()
    partners = [at(dx, dy) for dx, dy in CHIPS] + [at(dz=dz, dc=dc) for dz, dc in COLUMN]
    for partner in partners:
        pl.semaphore_signal(barrier, inc=1, device_id=partner, device_id_type=MESH)
    loads = []
    for q in range(4):
        cols = pl.ds(q * 1024, 1024)
        trio = [
            pltpu.make_async_copy(mom_hbm.at[:, cols], mom.at[:, cols], load_sem.at[q, 0]),
            pltpu.make_async_copy(grad_hbm.at[:, cols], grad.at[:, cols], load_sem.at[q, 1]),
            pltpu.make_async_copy(fac_hbm.at[cols, :], fac.at[cols, :], load_sem.at[q, 2]),
        ]
        for cp in trio:
            cp.start()
        loads.append(trio)

    part = None
    for q in range(4):
        for cp in loads[q]:
            cp.wait()
        cols = pl.ds(q * 1024, 1024)
        b = mom[:, cols] + grad[:, cols].astype(F32)
        mom[:, cols] = b
        p = dot3(split(b), split(fac[cols, :]), ((1,), (0,)))
        part = p if part is None else part + p
    zbuf[z] = part
    pl.semaphore_wait(barrier, len(partners))
    for dz in RING:
        send(zbuf.at[z], zbuf.at[z], z_sem.at[0], z_sem.at[1], at(dz=dz))
    z_all = group(zbuf.at[0:3], z_sem.at[0], z_sem.at[1])
    b_cp = send(mom.at[:, rows((1 - c) * HALF, HALF)], peer_b, b_sem.at[0], b_sem.at[1], at(dc=1))
    drains += [z_all, b_cp]
    z_all.wait_recv()
    left[0] = (zbuf[0] + zbuf[1]) + (zbuf[2] + zbuf[3])
    l_cp = send(left.at[0], left.at[1], l_sem.at[0], l_sem.at[1], at(dc=1))
    drains.append(l_cp)
    b_cp.wait_recv()
    l_cp.wait_recv()
    both = left[...].reshape(2 * ROWS, RANK)

    mine = left[:, :, rows(c * 128, 128)].reshape(2 * ROWS, 128)
    gsend[...] = dot6(mine, both, ((0,), (0,)))
    chip = y * 4 + x
    for i, (dx, dy) in enumerate(CHIPS):
        other = ((y + dy) % 4) * 4 + (x + dx) % 4
        send(gsend.at[rows(other * 8, 8), :], grecv.at[i], g_sem.at[0], g_sem.at[1], at(dx, dy))
    g_all = group(grecv, g_sem.at[0], g_sem.at[1])

    lh, ll = split(both)

    def product(start):
        own = mom[:, rows(c * HALF + start, BIG)]
        cat = jnp.concatenate([own, peer_b[:, rows(start, BIG)]], axis=0)
        gp[rows(start, BIG), :] = dot3(split(cat), (lh, ll), ((0,), (0,)))

    def step(h, d):
        return at(dx=d) if h == 0 else at(dy=d)

    def cross(h, d):
        return at(dy=d) if h == 0 else at(dx=d)

    along, across = (x, y), (y, x)
    both_h = (0, 1)

    def chunk(h, d):
        return h * QUARTER + ((along[h] + d) % 4) * BIG

    fwd_cps = {}
    for h in both_h:
        far = chunk(h, 2)
        product(far)
        for n, d in ((0, 1), (1, -1)):
            place = rows(far + n * 128, 128)
            fwd_cps[h, n] = send(gp.at[place, :], fwd.at[h, n], rs1_send.at[0], fwd_sem.at[h, n], step(h, d))
    for h in both_h:
        product(chunk(h, 1))
        product(chunk(h, -1))
    group(fwd, rs1_send.at[0], fwd_sem.at[0, 0]).wait_send()
    for h in both_h:
        for n, d in ((1, 1), (0, -1)):
            place = rows(chunk(h, d) + n * 128, 128)
            send(gp.at[place, :], rs1.at[h, 1 - n, n], rs1_send.at[1], rs1_sem.at[h], step(h, d))
    for h in both_h:
        product(chunk(h, 0))
    g_all.wait_recv()
    total = gsend[rows(chip * 8, 8), :]
    for i in range(len(CHIPS)):
        total = total + grecv[i]
    gown[...] = total
    gram[c * 16 + chip] = total
    for dx, dy in CHIPS:
        send(gown, gram.at[c * 16 + chip], gg_sem.at[0], gg_sem.at[1], at(dx, dy))
    gg_all = group(grecv, gg_sem.at[0], gg_sem.at[1])
    for h in both_h:
        for n, d in ((0, 1), (1, -1)):
            place = rows(chunk(h, d) + n * 128, 128)
            fwd_cps[h, n].wait_recv()
            gp[place, :] = gp[place, :] + fwd[h, n]
            send(gp.at[place, :], rs1.at[h, n, n], rs1_send.at[2], rs1_sem.at[h], step(h, d))
    gg_all.wait_recv()
    half_gram = gram.at[pl.ds(c * 16, 16)]
    core_gram = send(half_gram, half_gram, cg_sem.at[0], cg_sem.at[1], at(dc=1))
    drains += [g_all, gg_all, core_gram]

    for h in both_h:
        rs1_all = group(rs1.at[h], rs1_send.at[1 + h], rs1_sem.at[h])
        drains.append(rs1_all)
        rs1_all.wait_recv()
        mine = chunk(h, 0)
        for p in (0, 1):
            place = rows(mine + p * 128, 128)
            gp[place, :] = gp[place, :] + (rs1[h, 0, p] + rs1[h, 1, p])
        for i, d in enumerate((2, 1, 3)):
            place = rows(mine + ((across[h] + d) % 4) * SMALL, SMALL)
            send(gp.at[place, :], rs2.at[h, i], rs2_sem.at[h, 0], rs2_sem.at[h, 1], cross(h, d))
    core_gram.wait_recv()
    m[:, :RANK] = gram[...].reshape(RANK, RANK)
    r_id = lax.broadcasted_iota(jnp.int32, (RANK, RANK), 0)
    c_id = lax.broadcasted_iota(jnp.int32, (RANK, RANK), 1)
    m[:, RANK:] = jnp.where(r_id == c_id, 1.0, 0.0).astype(F32)
    factor_block(m, 0)
    for h in both_h:
        rs2_all = group(rs2.at[h], rs2_sem.at[h, 0], rs2_sem.at[h, 1])
        rs2_all.wait_recv()
        place = rows(chunk(h, 0) + across[h] * SMALL, SMALL)
        raw[place, :] = (gp[place, :] + rs2[h, 0]) + (rs2[h, 1] + rs2[h, 2])
        for d in (2, 1, 3):
            send(raw.at[place, :], raw.at[place, :], ag1_sem.at[h, 0], ag1_sem.at[h, 1], cross(h, d))
        drains += [rs2_all, group(rs2.at[h], ag1_sem.at[h, 0], ag1_sem.at[h, 1])]
    factor_block(m, 1)
    for h in both_h:
        drains[-1 if h else -3].wait_recv()
    ag2 = {}

    def gather(h, d, n, start):
        piece = raw.at[rows(start, 128), :]
        ag2[h, d, n] = send(piece, piece, ag2_send.at[n], ag2_sem.at[h, (1 - d) // 2, n], step(h, d))

    def gather_round(n):
        return group(raw.at[0:512], ag2_send.at[n], ag2_sem.at[0, 0, n])

    for h in both_h:
        gather(h, 1, 0, chunk(h, 0))
        gather(h, -1, 0, chunk(h, 0) + 128)
    factor_block(m, 2)
    gather_round(0).wait_send()
    for h in both_h:
        gather(h, 1, 1, chunk(h, 0) + 128)
        gather(h, -1, 1, chunk(h, 0))
    factor_block(m, 3)
    for h in both_h:
        ag2[h, 1, 0].wait_recv()
        gather(h, 1, 2, chunk(h, -1))
        ag2[h, -1, 0].wait_recv()
        gather(h, -1, 2, chunk(h, 1) + 128)
    drains += [gather_round(1), gather_round(2)]

    inverse = m[:, RANK:]
    inv = split(inverse)
    basis[...] = dot6(left[0], inverse, ((1,), (1,)))
    out_cps = [write(basis, basis_out, out_sem.at[0])]
    squares, pieces = [None], []

    def finish(g, start, size):
        r = dot3(split(raw[rows(start, size), :]), inv, ((1,), (1,)))
        mine = rows(c * HALF + start, size)
        right[mine, :] = r
        send(right.at[mine, :], right.at[mine, :], core_sem.at[g, 0], core_sem.at[g, 1], at(dc=1))
        write(right.at[mine, :], right_out.at[mine, :], out_sem.at[1])
        pieces.append((g, start, size))
        s = jnp.sum((r * r).reshape(size // 8, 8, RANK), axis=0)
        squares[0] = s if squares[0] is None else squares[0] + s

    for h in both_h:
        finish(0, chunk(h, 0), BIG)
    for h in both_h:
        finish(1, chunk(h, -1), 128)
        finish(1, chunk(h, 1) + 128, 128)
    for h in both_h:
        ag2[h, 1, 1].wait_recv()
        finish(2, chunk(h, -1) + 128, 128)
        ag2[h, -1, 1].wait_recv()
        finish(2, chunk(h, 1), 128)
    for h in both_h:
        ag2[h, 1, 2].wait_recv()
        finish(3, chunk(h, 2), 128)
        ag2[h, -1, 2].wait_recv()
        finish(3, chunk(h, 2) + 128, 128)
    sq_own[0:1, :] = jnp.sum(squares[0], axis=0, keepdims=True)
    for i, (dz, dc) in enumerate(COLUMN):
        send(sq_own.at[0:1], sq_in.at[i, 0:1], sq_sem.at[0], sq_sem.at[1], at(dz=dz, dc=dc))
    sq_all = group(sq_in.at[:, 0:1], sq_sem.at[0], sq_sem.at[1])
    drains.append(sq_all)
    for g in range(4):
        core_all = group(right.at[0:512], core_sem.at[g, 0], core_sem.at[g, 1])
        drains.append(core_all)
        core_all.wait_recv()
        for k, start, size in pieces:
            if k == g:
                theirs = rows((1 - c) * HALF + start, size)
                write(right.at[theirs, :], right_out.at[theirs, :], out_sem.at[1])
    sq_all.wait_recv()
    total = sq_own[0:1, :]
    for i in range(len(COLUMN)):
        total = total + sq_in[i, 0:1, :]
    norm[...] = jnp.broadcast_to(lax.rsqrt(total + 1e-06), (8, RANK))
    out_cps.append(write(norm, norm_out, out_sem.at[2]))
    out_cps.append(pltpu.make_async_copy(right, right_out, out_sem.at[1]))
    for cp in drains:
        cp.wait_send()
    for cp in out_cps:
        cp.wait()


def reduce_call(mom, grad, fac):
    vmem = pltpu.VMEM
    dma = pltpu.SemaphoreType.DMA
    return pl.pallas_call(
        reduce_kernel,
        out_shape=(
            jax.ShapeDtypeStruct((COLS, RANK), F32),
            jax.ShapeDtypeStruct((ROWS, RANK), F32),
            jax.ShapeDtypeStruct((8, RANK), F32),
        ),
        in_specs=[pl.BlockSpec(memory_space=pltpu.HBM)] * 3,
        out_specs=[pl.BlockSpec(memory_space=pl.ANY)] * 3,
        scratch_shapes=[
            vmem((ROWS, COLS), F32),
            vmem((ROWS, COLS), BF16),
            vmem((COLS, RANK), F32),
            vmem((ROWS, HALF), F32),
            vmem((NZ, ROWS, RANK), F32),
            vmem((2, ROWS, RANK), F32),
            vmem((128, RANK), F32),
            vmem((len(CHIPS), 8, RANK), F32),
            vmem((8, RANK), F32),
            vmem((32, 8, RANK), F32),
            vmem((RANK, 2 * RANK), F32),
            vmem((HALF, RANK), F32),
            vmem((2, 2, 128, RANK), F32),
            vmem((2, 2, 2, 128, RANK), F32),
            vmem((2, 3, SMALL, RANK), F32),
            vmem((HALF, RANK), F32),
            vmem((COLS, RANK), F32),
            vmem((ROWS, RANK), F32),
            vmem((8, RANK), F32),
            vmem((8, RANK), F32),
            vmem((len(COLUMN), 8, RANK), F32),
            dma((4, 3)),
            dma((2,)),
            dma((2,)),
            dma((2,)),
            dma((2,)),
            dma((2,)),
            dma((2,)),
            dma((2, 2)),
            dma((3,)),
            dma((2,)),
            dma((2, 2)),
            dma((2, 2)),
            dma((3,)),
            dma((2, 2, 3)),
            dma((4, 2)),
            dma((2,)),
            dma((3,)),
        ],
        compiler_params=pltpu.CompilerParams(
            collective_id=0, has_side_effects=True, vmem_limit_bytes=32 * 2**20
        ),
    )(mom, grad, fac)


def update_kernel(
    scal, w, mom, grad, right, basis, norm, new_w_out, new_mom_out, new_fac_out, new_w, new_mom, new_fac, sem
):
    decay, rate = scal[0], scal[1]
    s = norm[0:1, :]
    q = basis[...]
    scale = rate * jnp.sqrt(jnp.float32(4096 * 16384 / RANK))
    stacked = split(jnp.concatenate([q * (1.0 - decay), q * (s * scale)], axis=0))
    wide = 512
    for i in range(COLS // wide):
        at = pl.ds(i * wide, wide)
        r = right[at, :]
        new_fac[at, :] = r * s
        pltpu.make_async_copy(new_fac.at[at, :], new_fac_out.at[at, :], sem.at[2]).start()
        d = dot3(stacked, split(r), ((1,), (1,)))
        new_mom[:, at] = (mom[:, at] + grad[:, at].astype(F32)) - d[:ROWS]
        pltpu.make_async_copy(new_mom.at[:, at], new_mom_out.at[:, at], sem.at[1]).start()
        new_w[:, at] = w[:, at] - d[ROWS:]
        pltpu.make_async_copy(new_w.at[:, at], new_w_out.at[:, at], sem.at[0]).start()
    pltpu.make_async_copy(new_w, new_w_out, sem.at[0]).wait()
    pltpu.make_async_copy(new_mom, new_mom_out, sem.at[1]).wait()
    pltpu.make_async_copy(new_fac, new_fac_out, sem.at[2]).wait()


def update_call(scal, w, mom, grad, right, basis, norm):
    here = pl.BlockSpec(memory_space=pltpu.VMEM)
    outs = [(ROWS, COLS), (ROWS, COLS), (COLS, RANK)]
    return pl.pallas_call(
        update_kernel,
        out_shape=[jax.ShapeDtypeStruct(shape, F32) for shape in outs],
        in_specs=[pl.BlockSpec(memory_space=pltpu.SMEM)] + [here] * 6,
        out_specs=[pl.BlockSpec(memory_space=pl.ANY)] * 3,
        scratch_shapes=[pltpu.VMEM(shape, F32) for shape in outs] + [pltpu.SemaphoreType.DMA((3,))],
        compiler_params=pltpu.CompilerParams(vmem_limit_bytes=24 * 2**20),
    )(scal, w, mom, grad, right, basis, norm)


def body(weight, momentum, gradient, factor, decay, rate):
    keep = [pltpu.with_memory_space_constraint(a, pltpu.HBM) for a in (momentum, gradient, factor)]
    right, basis, norm = reduce_call(*keep)
    scal = jnp.stack([decay, rate])
    return tuple(update_call(scal, weight, momentum, gradient, right, basis, norm))


def solution(mesh):
    placed = (P("fsdp", "tp"), P("fsdp", "tp"), P("fsdp", "tp"), P("tp", None), P(), P())
    return jax.shard_map(
        body,
        mesh=mesh,
        in_specs=placed,
        out_specs=(P("fsdp", "tp"), P("fsdp", "tp"), P("tp", None)),
        check_vma=False,
    )
```

```python
import jax
import jax.numpy as jnp
from jax import lax
from jax.experimental import pallas as pl
from jax.experimental.pallas import tpu as pltpu
from jax.sharding import PartitionSpec as P

F32 = jnp.float32
BF16 = jnp.bfloat16
HIGH = lax.Precision.HIGHEST
MESH = pl.DeviceIdType.MESH
NX = NY = NZ = 4
ROWS, COLS, RANK = 128, 4096, 256
HALF = COLS // 2
QUARTER = HALF // 2
BIG = QUARTER // 4
SMALL = BIG // 4
CHIPS = [(dx, dy) for dx in range(NX) for dy in range(NY) if dx or dy]
RING = (1, 3, 2)
COLUMN = [(dz, dc) for dz in range(NZ) for dc in range(2) if dz or dc]


def split(x):
    hi = x.astype(BF16)
    return hi, (x - hi.astype(F32)).astype(BF16)


def dot3(a, b, dims):
    (ah, al), (bh, bl) = a, b

    def one(p, q):
        return lax.dot_general(p, q, (dims, ((), ())), preferred_element_type=F32)

    return one(ah, bh) + (one(ah, bl) + one(al, bh))


def dot6(a, b, dims):
    return lax.dot_general(a, b, (dims, ((), ())), precision=HIGH, preferred_element_type=F32)


def row_of(t, s):
    return jnp.broadcast_to(t[s : s + 1, :], (8, 128))


def lane_of(t, l):
    return jnp.broadcast_to(t[:, l : l + 1], (8, 128))


def eliminate(d):
    nb, nt = 64, 8
    lane = lax.broadcasted_iota(jnp.int32, (8, 128), 1)
    sub = lax.broadcasted_iota(jnp.int32, (8, 128), 0)
    w = []
    for i in range(nt):
        tile = jnp.concatenate([d[8 * i : 8 * i + 8, :], jnp.zeros((8, 128 - nb), F32)], axis=1)
        w.append(jnp.where(lane == nb + 8 * i + sub, 1.0, tile))
    out = []
    for k in range(nt):
        tile = w[k]
        cs = [lane_of(tile, 8 * k + j) for j in range(8)]
        others = [[lane_of(w[i], 8 * k + j) for j in range(8)] for i in range(k + 1, nt)]
        v = tile
        for p in range(8):
            piv = row_of(cs[p], p)
            inv = 1.0 / piv
            row = row_of(tile, p)
            mine = sub == p
            v = jnp.where(mine, row * lax.rsqrt(piv), v)
            rn = row * inv
            cz = jnp.where(mine, 0.0, cs[p])
            tile = jnp.where(mine, rn, tile) - cz * rn
            for j in range(p + 1, 8):
                rj = row_of(cs[j], p) * inv
                cs[j] = jnp.where(mine, rj, cs[j]) - cz * rj
        out.append(v)
        if k + 1 < nt:
            ts = [row_of(tile, p) for p in range(8)]
            for i in range(k + 1, nt):
                acc = [others[i - k - 1][p] * ts[p] for p in range(8)]
                while len(acc) > 1:
                    acc = [acc[q] + acc[q + 1] for q in range(0, len(acc), 2)]
                w[i] = w[i] - acc[0]
    return jnp.concatenate([o[:, nb : 2 * nb] for o in out], axis=0)


def inverse_block(m, k):
    return eliminate(m[64 * k : 64 * k + 64, 64 * k : 64 * k + 64])


def factor_block(m, k, inv):
    lo, hi = 64 * k, 64 * k + 64
    v = dot6(inv, m[lo:hi, :], ((1,), (0,)))
    m[lo:hi, :] = v
    if hi < RANK:
        ut = v[:, :RANK].T[hi:, :]
        m[hi:, :] -= dot6(ut, v, ((1,), (0,)))


def reduce_kernel(
    mom_hbm, grad_hbm, fac_hbm, right_out, basis_out, norm_out,
    mom, grad, fac, peer_b, zbuf, left, gsend, grecv, gown, gram, m, gp, fwd, rs1, rs2, raw, right, basis, norm, sq_own, sq_in,
    load_sem, b_sem, z_sem, l_sem, g_sem, gg_sem, cg_sem, fwd_sem, rs1_send, rs1_sem, rs2_sem, ag1_sem, ag2_send, ag2_sem,
    core_sem, sq_sem, out_sem,
):
    f = lax.axis_index("fsdp")
    z = lax.axis_index("tp")
    y, x, c = f // 8, (f // 2) % 4, f % 2

    def fence():
        @pl.when(z < 0)
        def _():
            gown[...] = gown[...] + 1.0

    def at(dx=0, dy=0, dc=0, dz=0):
        return ((((y + dy) % 4) * 4 + (x + dx) % 4) * 2 + (c + dc) % 2, (z + dz) % 4)

    def copy(src, dst, send_sem, recv_sem, where):
        return pltpu.make_async_remote_copy(
            src, dst, send_sem, recv_sem, device_id=where, device_id_type=MESH
        )

    drains = []

    def send(src, dst, send_sem, recv_sem, where):
        cp = copy(src, dst, send_sem, recv_sem, where)
        cp.start()
        return cp

    def group(ref, send_sem, recv_sem):
        return copy(ref, ref, send_sem, recv_sem, at(dc=1))

    def write(src, dst, sem):
        cp = pltpu.make_async_copy(src, dst, sem)
        cp.start()
        return cp

    def rows(start, size):
        return pl.ds(pl.multiple_of(start, size), size)

    fence()
    barrier = pltpu.get_barrier_semaphore()
    partners = [at(dx, dy) for dx, dy in CHIPS] + [at(dz=dz, dc=dc) for dz, dc in COLUMN]
    for partner in partners:
        pl.semaphore_signal(barrier, inc=1, device_id=partner, device_id_type=MESH)
    loads = []
    for q in range(4):
        cols = pl.ds(q * 1024, 1024)
        trio = [
            pltpu.make_async_copy(mom_hbm.at[:, cols], mom.at[:, cols], load_sem.at[q, 0]),
            pltpu.make_async_copy(grad_hbm.at[:, cols], grad.at[:, cols], load_sem.at[q, 1]),
            pltpu.make_async_copy(fac_hbm.at[cols, :], fac.at[cols, :], load_sem.at[q, 2]),
        ]
        for cp in trio:
            cp.start()
        loads.append(trio)

    fence()
    part = None
    for q in range(4):
        for cp in loads[q]:
            cp.wait()
        cols = pl.ds(q * 1024, 1024)
        b = mom[:, cols] + grad[:, cols].astype(F32)
        mom[:, cols] = b
        p = dot3(split(b), split(fac[cols, :]), ((1,), (0,)))
        part = p if part is None else part + p
    zbuf[z] = part
    fence()
    pl.semaphore_wait(barrier, len(partners))
    fence()
    for dz in RING:
        send(zbuf.at[z], zbuf.at[z], z_sem.at[0], z_sem.at[1], at(dz=dz))
    z_all = group(zbuf.at[0:3], z_sem.at[0], z_sem.at[1])
    b_cp = send(mom.at[:, rows((1 - c) * HALF, HALF)], peer_b, b_sem.at[0], b_sem.at[1], at(dc=1))
    drains += [z_all, b_cp]
    fence()
    z_all.wait_recv()
    left[0] = (zbuf[0] + zbuf[1]) + (zbuf[2] + zbuf[3])
    l_cp = send(left.at[0], left.at[1], l_sem.at[0], l_sem.at[1], at(dc=1))
    drains.append(l_cp)
    b_cp.wait_recv()
    fence()
    l_cp.wait_recv()
    both = left[...].reshape(2 * ROWS, RANK)

    fence()
    mine = left[:, :, rows(c * 128, 128)].reshape(2 * ROWS, 128)
    gsend[...] = dot6(mine, both, ((0,), (0,)))
    fence()
    chip = y * 4 + x
    for i, (dx, dy) in enumerate(CHIPS):
        other = ((y + dy) % 4) * 4 + (x + dx) % 4
        send(gsend.at[rows(other * 8, 8), :], grecv.at[i], g_sem.at[0], g_sem.at[1], at(dx, dy))
    g_all = group(grecv, g_sem.at[0], g_sem.at[1])

    fence()
    lh, ll = split(both)

    def product(start):
        own = mom[:, rows(c * HALF + start, BIG)]
        cat = jnp.concatenate([own, peer_b[:, rows(start, BIG)]], axis=0)
        gp[rows(start, BIG), :] = dot3(split(cat), (lh, ll), ((0,), (0,)))

    def step(h, d):
        return at(dx=d) if h == 0 else at(dy=d)

    def cross(h, d):
        return at(dy=d) if h == 0 else at(dx=d)

    along, across = (x, y), (y, x)
    both_h = (0, 1)

    def chunk(h, d):
        return h * QUARTER + ((along[h] + d) % 4) * BIG

    fwd_cps = {}
    for h in both_h:
        far = chunk(h, 2)
        product(far)
        for n, d in ((0, 1), (1, -1)):
            place = rows(far + n * 128, 128)
            fwd_cps[h, n] = send(gp.at[place, :], fwd.at[h, n], rs1_send.at[0], fwd_sem.at[h, n], step(h, d))
    for h in both_h:
        product(chunk(h, 1))
        product(chunk(h, -1))
    for h in both_h:
        product(chunk(h, 0))
    fence()
    for h in both_h:
        for n, d in ((1, 1), (0, -1)):
            place = rows(chunk(h, d) + n * 128, 128)
            send(gp.at[place, :], rs1.at[h, 1 - n, n], rs1_send.at[1], rs1_sem.at[h], step(h, d))
    drains.append(group(fwd, rs1_send.at[0], fwd_sem.at[0, 0]))
    fence()
    for h in both_h:
        for n, d in ((0, 1), (1, -1)):
            place = rows(chunk(h, d) + n * 128, 128)
            fwd_cps[h, n].wait_recv()
            gp[place, :] = gp[place, :] + fwd[h, n]
            send(gp.at[place, :], rs1.at[h, n, n], rs1_send.at[2], rs1_sem.at[h], step(h, d))
    fence()
    g_all.wait_recv()
    total = gsend[rows(chip * 8, 8), :]
    for i in range(len(CHIPS)):
        total = total + grecv[i]
    fence()
    gown[...] = total
    gram[c * 16 + chip] = total
    for dx, dy in CHIPS:
        send(gown, gram.at[c * 16 + chip], gg_sem.at[0], gg_sem.at[1], at(dx, dy))
    gg_all = group(grecv, gg_sem.at[0], gg_sem.at[1])
    drains += [g_all, gg_all]

    fence()
    for h in both_h:
        rs1_all = group(rs1.at[h], rs1_send.at[1 + h], rs1_sem.at[h])
        drains.append(rs1_all)
        rs1_all.wait_recv()
        mine = chunk(h, 0)
        for p in (0, 1):
            place = rows(mine + p * 128, 128)
            gp[place, :] = gp[place, :] + (rs1[h, 0, p] + rs1[h, 1, p])
        for i, d in enumerate((2, 1, 3)):
            place = rows(mine + ((across[h] + d) % 4) * SMALL, SMALL)
            send(gp.at[place, :], rs2.at[h, i], rs2_sem.at[h, 0], rs2_sem.at[h, 1], cross(h, d))
    fence()
    gg_all.wait_recv()
    half_gram = gram.at[pl.ds(c * 16, 16)]
    core_gram = send(half_gram, half_gram, cg_sem.at[0], cg_sem.at[1], at(dc=1))
    drains.append(core_gram)
    r_id = lax.broadcasted_iota(jnp.int32, (RANK, RANK), 0)
    c_id = lax.broadcasted_iota(jnp.int32, (RANK, RANK), 1)
    m[:, RANK:] = jnp.where(r_id == c_id, 1.0, 0.0).astype(F32)
    fence()
    core_gram.wait_recv()
    m[:, :RANK] = gram[...].reshape(RANK, RANK)
    fence()
    inv0 = inverse_block(m, 0)
    fence()
    ag1_all = []
    for h in both_h:
        rs2_all = group(rs2.at[h], rs2_sem.at[h, 0], rs2_sem.at[h, 1])
        rs2_all.wait_recv()
        place = rows(chunk(h, 0) + across[h] * SMALL, SMALL)
        raw[place, :] = (gp[place, :] + rs2[h, 0]) + (rs2[h, 1] + rs2[h, 2])
        for d in (2, 1, 3):
            send(raw.at[place, :], raw.at[place, :], ag1_sem.at[h, 0], ag1_sem.at[h, 1], cross(h, d))
        ag1_all.append(group(rs2.at[h], ag1_sem.at[h, 0], ag1_sem.at[h, 1]))
        drains += [rs2_all, ag1_all[h]]
    fence()
    factor_block(m, 0, inv0)
    factor_block(m, 1, inverse_block(m, 1))
    fence()
    for cp in ag1_all:
        cp.wait_recv()
    ag2 = {}

    def gather(h, d, n, start):
        piece = raw.at[rows(start, 128), :]
        ag2[h, d, n] = send(piece, piece, ag2_send.at[n], ag2_sem.at[h, (1 - d) // 2, n], step(h, d))

    def gather_round(n):
        return group(raw.at[0:512], ag2_send.at[n], ag2_sem.at[0, 0, n])

    for h in both_h:
        gather(h, 1, 0, chunk(h, 0))
        gather(h, -1, 0, chunk(h, 0) + 128)
    fence()
    factor_block(m, 2, inverse_block(m, 2))
    fence()
    for h in both_h:
        gather(h, 1, 1, chunk(h, 0) + 128)
        gather(h, -1, 1, chunk(h, 0))
    fence()
    factor_block(m, 3, inverse_block(m, 3))
    fence()
    for h in both_h:
        ag2[h, 1, 0].wait_recv()
        gather(h, 1, 2, chunk(h, -1))
        ag2[h, -1, 0].wait_recv()
        gather(h, -1, 2, chunk(h, 1) + 128)
    drains += [gather_round(n) for n in range(3)]

    fence()
    upper = m[:, RANK:].T
    inv = split(upper)
    squares, pieces = [None], []

    def finish(g, start, size):
        r = dot3(split(raw[rows(start, size), :]), inv, ((1,), (0,)))
        mine = rows(c * HALF + start, size)
        right[mine, :] = r
        send(right.at[mine, :], right.at[mine, :], core_sem.at[g, 0], core_sem.at[g, 1], at(dc=1))
        write(right.at[mine, :], right_out.at[mine, :], out_sem.at[1])
        pieces.append((g, start, size))
        s = jnp.sum((r * r).reshape(size // 8, 8, RANK), axis=0)
        squares[0] = s if squares[0] is None else squares[0] + s

    for h in both_h:
        finish(0, chunk(h, 0), BIG)
    basis[...] = dot6(left[0], upper, ((1,), (0,)))
    out_cps = [write(basis, basis_out, out_sem.at[0])]
    for h in both_h:
        finish(1, chunk(h, -1), 128)
        finish(1, chunk(h, 1) + 128, 128)
    fence()
    for h in both_h:
        ag2[h, 1, 1].wait_recv()
        finish(2, chunk(h, -1) + 128, 128)
        ag2[h, -1, 1].wait_recv()
        finish(2, chunk(h, 1), 128)
    fence()
    for h in both_h:
        ag2[h, 1, 2].wait_recv()
        finish(3, chunk(h, 2), 128)
        ag2[h, -1, 2].wait_recv()
        finish(3, chunk(h, 2) + 128, 128)
    fence()
    sq_own[0:1, :] = jnp.sum(squares[0], axis=0, keepdims=True)
    for i, (dz, dc) in enumerate(COLUMN):
        send(sq_own.at[0:1], sq_in.at[i, 0:1], sq_sem.at[0], sq_sem.at[1], at(dz=dz, dc=dc))
    sq_all = group(sq_in.at[:, 0:1], sq_sem.at[0], sq_sem.at[1])
    drains.append(sq_all)
    fence()
    for g in range(4):
        core_all = group(right.at[0:512], core_sem.at[g, 0], core_sem.at[g, 1])
        drains.append(core_all)
        core_all.wait_recv()
        for k, start, size in pieces:
            if k == g:
                theirs = rows((1 - c) * HALF + start, size)
                write(right.at[theirs, :], right_out.at[theirs, :], out_sem.at[1])
    fence()
    sq_all.wait_recv()
    total = sq_own[0:1, :]
    for i in range(len(COLUMN)):
        total = total + sq_in[i, 0:1, :]
    norm[...] = jnp.broadcast_to(lax.rsqrt(total + 1e-06), (8, RANK))
    out_cps.append(write(norm, norm_out, out_sem.at[2]))
    out_cps.append(pltpu.make_async_copy(right, right_out, out_sem.at[1]))
    fence()
    for cp in drains:
        cp.wait_send()
    for cp in out_cps:
        cp.wait()


def reduce_call(mom, grad, fac):
    vmem = pltpu.VMEM
    dma = pltpu.SemaphoreType.DMA
    return pl.pallas_call(
        reduce_kernel,
        out_shape=(
            jax.ShapeDtypeStruct((COLS, RANK), F32),
            jax.ShapeDtypeStruct((ROWS, RANK), F32),
            jax.ShapeDtypeStruct((8, RANK), F32),
        ),
        in_specs=[pl.BlockSpec(memory_space=pltpu.HBM)] * 3,
        out_specs=[pl.BlockSpec(memory_space=pl.ANY)] * 3,
        scratch_shapes=[
            vmem((ROWS, COLS), F32),
            vmem((ROWS, COLS), BF16),
            vmem((COLS, RANK), F32),
            vmem((ROWS, HALF), F32),
            vmem((NZ, ROWS, RANK), F32),
            vmem((2, ROWS, RANK), F32),
            vmem((128, RANK), F32),
            vmem((len(CHIPS), 8, RANK), F32),
            vmem((8, RANK), F32),
            vmem((32, 8, RANK), F32),
            vmem((RANK, 2 * RANK), F32),
            vmem((HALF, RANK), F32),
            vmem((2, 2, 128, RANK), F32),
            vmem((2, 2, 2, 128, RANK), F32),
            vmem((2, 3, SMALL, RANK), F32),
            vmem((HALF, RANK), F32),
            vmem((COLS, RANK), F32),
            vmem((ROWS, RANK), F32),
            vmem((8, RANK), F32),
            vmem((8, RANK), F32),
            vmem((len(COLUMN), 8, RANK), F32),
            dma((4, 3)),
            dma((2,)),
            dma((2,)),
            dma((2,)),
            dma((2,)),
            dma((2,)),
            dma((2,)),
            dma((2, 2)),
            dma((3,)),
            dma((2,)),
            dma((2, 2)),
            dma((2, 2)),
            dma((3,)),
            dma((2, 2, 3)),
            dma((4, 2)),
            dma((2,)),
            dma((3,)),
        ],
        compiler_params=pltpu.CompilerParams(
            collective_id=0, has_side_effects=True, vmem_limit_bytes=32 * 2**20
        ),
    )(mom, grad, fac)


def update_kernel(
    scal, w, mom, grad, right, basis, norm, new_w_out, new_mom_out, new_fac_out, new_w, new_mom, new_fac, sem
):
    decay, rate = scal[0], scal[1]
    s = norm[0:1, :]
    q = basis[...]
    scale = rate * jnp.sqrt(jnp.float32(4096 * 16384 / RANK))
    stacked = split(jnp.concatenate([q * (1.0 - decay), q * (s * scale)], axis=0))
    wide = 512
    for i in range(COLS // wide):
        at = pl.ds(i * wide, wide)
        r = right[at, :]
        new_fac[at, :] = r * s
        pltpu.make_async_copy(new_fac.at[at, :], new_fac_out.at[at, :], sem.at[2]).start()
        d = dot3(stacked, split(r), ((1,), (1,)))
        new_mom[:, at] = (mom[:, at] + grad[:, at].astype(F32)) - d[:ROWS]
        pltpu.make_async_copy(new_mom.at[:, at], new_mom_out.at[:, at], sem.at[1]).start()
        new_w[:, at] = w[:, at] - d[ROWS:]
        pltpu.make_async_copy(new_w.at[:, at], new_w_out.at[:, at], sem.at[0]).start()
    pltpu.make_async_copy(new_w, new_w_out, sem.at[0]).wait()
    pltpu.make_async_copy(new_mom, new_mom_out, sem.at[1]).wait()
    pltpu.make_async_copy(new_fac, new_fac_out, sem.at[2]).wait()


def update_call(scal, w, mom, grad, right, basis, norm):
    here = pl.BlockSpec(memory_space=pltpu.VMEM)
    outs = [(ROWS, COLS), (ROWS, COLS), (COLS, RANK)]
    return pl.pallas_call(
        update_kernel,
        out_shape=[jax.ShapeDtypeStruct(shape, F32) for shape in outs],
        in_specs=[pl.BlockSpec(memory_space=pltpu.SMEM)] + [here] * 6,
        out_specs=[pl.BlockSpec(memory_space=pl.ANY)] * 3,
        scratch_shapes=[pltpu.VMEM(shape, F32) for shape in outs] + [pltpu.SemaphoreType.DMA((3,))],
        compiler_params=pltpu.CompilerParams(vmem_limit_bytes=24 * 2**20),
    )(scal, w, mom, grad, right, basis, norm)


def body(weight, momentum, gradient, factor, decay, rate):
    keep = [pltpu.with_memory_space_constraint(a, pltpu.HBM) for a in (momentum, gradient, factor)]
    right, basis, norm = reduce_call(*keep)
    scal = jnp.stack([decay, rate])
    return tuple(update_call(scal, weight, momentum, gradient, right, basis, norm))


def solution(mesh):
    placed = (P("fsdp", "tp"), P("fsdp", "tp"), P("fsdp", "tp"), P("tp", None), P(), P())
    return jax.shard_map(
        body,
        mesh=mesh,
        in_specs=placed,
        out_specs=(P("fsdp", "tp"), P("fsdp", "tp"), P("tp", None)),
        check_vma=False,
    )
```

```python
import jax
import jax.numpy as jnp
from jax import lax
from jax.experimental import pallas as pl
from jax.experimental.pallas import tpu as pltpu
from jax.sharding import PartitionSpec as P

F32 = jnp.float32
BF16 = jnp.bfloat16
HIGH = lax.Precision.HIGHEST
MESH = pl.DeviceIdType.MESH
NX = NY = NZ = 4
ROWS, COLS, RANK = 128, 4096, 256
HALF = COLS // 2
QUARTER = HALF // 2
BIG = QUARTER // 4
SMALL = BIG // 4
CHIPS = [(dx, dy) for dx in range(NX) for dy in range(NY) if dx or dy]
RING = (1, 3, 2)
COLUMN = [(dz, dc) for dz in range(NZ) for dc in range(2) if dz or dc]


def split(x):
    hi = x.astype(BF16)
    return hi, (x - hi.astype(F32)).astype(BF16)


def dot3(a, b, dims):
    (ah, al), (bh, bl) = a, b

    def one(p, q):
        return lax.dot_general(p, q, (dims, ((), ())), preferred_element_type=F32)

    if dims[0] == (1,):
        n = ah.shape[0]
        both = one(jnp.concatenate([ah, al], axis=0), bh)
        return both[:n] + (both[n:] + one(ah, bl))
    return one(ah, bh) + (one(ah, bl) + one(al, bh))


def dot6(a, b, dims):
    return lax.dot_general(a, b, (dims, ((), ())), precision=HIGH, preferred_element_type=F32)


def row_of(t, s):
    return jnp.broadcast_to(t[s : s + 1, :], (8, 128))


def lane_of(t, l):
    return jnp.broadcast_to(t[:, l : l + 1], (8, 128))


def eliminate(d, between=None):
    nb, nt = 64, 8
    lane = lax.broadcasted_iota(jnp.int32, (8, 128), 1)
    sub = lax.broadcasted_iota(jnp.int32, (8, 128), 0)
    w = []
    for i in range(nt):
        tile = jnp.concatenate([d[8 * i : 8 * i + 8, :], jnp.zeros((8, 128 - nb), F32)], axis=1)
        w.append(jnp.where(lane == nb + 8 * i + sub, 1.0, tile))
    out = []
    for k in range(nt):
        if k == nt // 2 and between is not None:
            between()
        tile = w[k]
        cs = [lane_of(tile, 8 * k + j) for j in range(8)]
        others = [[lane_of(w[i], 8 * k + j) for j in range(8)] for i in range(k + 1, nt)]
        v = tile
        for p in range(8):
            piv = row_of(cs[p], p)
            inv = 1.0 / piv
            row = row_of(tile, p)
            mine = sub == p
            v = jnp.where(mine, row * lax.rsqrt(piv), v)
            rn = row * inv
            cz = jnp.where(mine, 0.0, cs[p])
            tile = jnp.where(mine, rn, tile) - cz * rn
            for j in range(p + 1, 8):
                rj = row_of(cs[j], p) * inv
                cs[j] = jnp.where(mine, rj, cs[j]) - cz * rj
        out.append(v)
        if k + 1 < nt:
            ts = [row_of(tile, p) for p in range(8)]
            for i in range(k + 1, nt):
                acc = [others[i - k - 1][p] * ts[p] for p in range(8)]
                while len(acc) > 1:
                    acc = [acc[q] + acc[q + 1] for q in range(0, len(acc), 2)]
                w[i] = w[i] - acc[0]
    return jnp.concatenate([o[:, nb : 2 * nb] for o in out], axis=0)


def inverse_block(m, k, between=None):
    return eliminate(m[64 * k : 64 * k + 64, 64 * k : 64 * k + 64], between)


def factor_block(m, k, inv):
    lo, hi = 64 * k, 64 * k + 64
    v = dot6(inv, m[lo:hi, :], ((1,), (0,)))
    m[lo:hi, :] = v
    if hi < RANK:
        ut = v[:, :RANK].T[hi:, :]
        m[hi:, :] -= dot6(ut, v, ((1,), (0,)))


def reduce_kernel(
    mom_hbm, grad_hbm, fac_hbm, w_hbm, right, basis, norm, mom, w,
    grad, fac, peer_b, turned, zbuf, left, gsend, grecv, gown, gram, m, gp, fwd, rs1, rs2, raw, sq_own, sq_in, sq_sum, sq_end,
    load_sem, b_sem, z_sem, l_sem, g_sem, gg_sem, cg_sem, fwd_sem, rs1_send, rs1_sem, rs2_sem, ag1_sem, ag2_send, ag2_sem,
    core_sem, sq_sem, sqe_sem, w_sem,
):
    f = lax.axis_index("fsdp")
    z = lax.axis_index("tp")
    y, x, c = f // 8, (f // 2) % 4, f % 2

    def fence():
        @pl.when(z < 0)
        def _():
            gown[...] = gown[...] + 1.0

    def at(dx=0, dy=0, dc=0, dz=0):
        return ((((y + dy) % 4) * 4 + (x + dx) % 4) * 2 + (c + dc) % 2, (z + dz) % 4)

    def copy(src, dst, send_sem, recv_sem, where):
        return pltpu.make_async_remote_copy(
            src, dst, send_sem, recv_sem, device_id=where, device_id_type=MESH
        )

    drains = []

    def send(src, dst, send_sem, recv_sem, where):
        cp = copy(src, dst, send_sem, recv_sem, where)
        cp.start()
        return cp

    def group(ref, send_sem, recv_sem):
        return copy(ref, ref, send_sem, recv_sem, at(dc=1))

    def write(src, dst, sem):
        cp = pltpu.make_async_copy(src, dst, sem)
        cp.start()
        return cp

    def rows(start, size):
        return pl.ds(pl.multiple_of(start, size), size)

    fence()
    barrier = pltpu.get_barrier_semaphore()
    partners = [at(dx, dy) for dx, dy in CHIPS] + [at(dz=dz, dc=dc) for dz, dc in COLUMN]
    for partner in partners:
        pl.semaphore_signal(barrier, inc=1, device_id=partner, device_id_type=MESH)
    blocks, ahead = 4, 4
    wide = COLS // blocks

    def load(q):
        cols = pl.ds(q * wide, wide)
        trio = [
            pltpu.make_async_copy(mom_hbm.at[:, cols], mom.at[:, cols], load_sem.at[q, 0]),
            pltpu.make_async_copy(grad_hbm.at[:, cols], grad.at[:, cols], load_sem.at[q, 1]),
            pltpu.make_async_copy(fac_hbm.at[cols, :], fac.at[cols, :], load_sem.at[q, 2]),
        ]
        for cp in trio:
            cp.start()
        return trio

    loads = [load(q) for q in range(ahead)]

    fence()
    part = None
    for q in range(blocks):
        for cp in loads[q]:
            cp.wait()
        if q + ahead < blocks:
            loads.append(load(q + ahead))
        cols = pl.ds(q * wide, wide)
        b = mom[:, cols] + grad[:, cols].astype(F32)
        mom[:, cols] = b
        p = dot3(split(b), split(fac[cols, :]), ((1,), (0,)))
        part = p if part is None else part + p
    zbuf[z] = part
    fence()
    pl.semaphore_wait(barrier, len(partners))
    fence()
    for dz in RING:
        send(zbuf.at[z], zbuf.at[z], z_sem.at[0], z_sem.at[1], at(dz=dz))
    z_all = group(zbuf.at[0:3], z_sem.at[0], z_sem.at[1])
    b_cp = send(mom.at[:, rows((1 - c) * HALF, HALF)], peer_b, b_sem.at[0], b_sem.at[1], at(dc=1))
    drains += [z_all, b_cp]
    w_cp = write(w_hbm, w, w_sem.at[0])
    fence()
    b_cp.wait_recv()
    for i in range(HALF // BIG):
        part = jnp.concatenate([mom[:, rows(c * HALF + i * BIG, BIG)], peer_b[:, i * BIG : (i + 1) * BIG]], axis=0)
        hi, lo = split(part.T)
        turned[0, i * BIG : (i + 1) * BIG, :] = hi
        turned[1, i * BIG : (i + 1) * BIG, :] = lo
    fence()
    z_all.wait_recv()
    left[0] = (zbuf[0] + zbuf[1]) + (zbuf[2] + zbuf[3])
    l_cp = send(left.at[0], left.at[1], l_sem.at[0], l_sem.at[1], at(dc=1))
    drains.append(l_cp)
    fence()
    l_cp.wait_recv()
    both = left[...].reshape(2 * ROWS, RANK)

    fence()
    lh, ll = split(both)

    def product(start):
        place = rows(start, BIG)
        gp[place, :] = dot3((turned[0, place, :], turned[1, place, :]), (lh, ll), ((1,), (0,)))

    def step(h, d):
        return at(dx=d) if h == 0 else at(dy=d)

    def cross(h, d):
        return at(dy=d) if h == 0 else at(dx=d)

    along, across = (x, y), (y, x)
    both_h = (0, 1)

    def chunk(h, d):
        return h * QUARTER + ((along[h] + d) % 4) * BIG

    fwd_cps = {}
    for h in both_h:
        far = chunk(h, 2)
        product(far)
        for n, d in ((0, 1), (1, -1)):
            place = rows(far + n * 128, 128)
            fwd_cps[h, n] = send(gp.at[place, :], fwd.at[h, n], rs1_send.at[0], fwd_sem.at[h, n], step(h, d))
    fence()
    mine = left[:, :, rows(c * 128, 128)].reshape(2 * ROWS, 128)
    gsend[...] = dot6(mine, both, ((0,), (0,)))
    fence()
    chip = y * 4 + x
    for i, (dx, dy) in enumerate(CHIPS):
        other = ((y + dy) % 4) * 4 + (x + dx) % 4
        send(gsend.at[rows(other * 8, 8), :], grecv.at[i], g_sem.at[0], g_sem.at[1], at(dx, dy))
    g_all = group(grecv, g_sem.at[0], g_sem.at[1])

    fence()
    for h in both_h:
        product(chunk(h, 1))
        product(chunk(h, -1))
    for h in both_h:
        product(chunk(h, 0))
    fence()
    for h in both_h:
        for n, d in ((1, 1), (0, -1)):
            place = rows(chunk(h, d) + n * 128, 128)
            send(gp.at[place, :], rs1.at[h, 1 - n, n], rs1_send.at[1], rs1_sem.at[h], step(h, d))
    drains.append(group(fwd, rs1_send.at[0], fwd_sem.at[0, 0]))
    fence()
    for h in both_h:
        for n, d in ((0, 1), (1, -1)):
            place = rows(chunk(h, d) + n * 128, 128)
            fwd_cps[h, n].wait_recv()
            gp[place, :] = gp[place, :] + fwd[h, n]
            send(gp.at[place, :], rs1.at[h, n, n], rs1_send.at[2], rs1_sem.at[h], step(h, d))
    fence()
    g_all.wait_recv()
    total = gsend[rows(chip * 8, 8), :]
    for i in range(len(CHIPS)):
        total = total + grecv[i]
    fence()
    gown[...] = total
    gram[c * 16 + chip] = total
    for dx, dy in CHIPS:
        send(gown, gram.at[c * 16 + chip], gg_sem.at[0], gg_sem.at[1], at(dx, dy))
    gg_all = group(grecv, gg_sem.at[0], gg_sem.at[1])
    drains += [g_all, gg_all]

    fence()
    for h in both_h:
        rs1_all = group(rs1.at[h], rs1_send.at[1 + h], rs1_sem.at[h])
        drains.append(rs1_all)
        rs1_all.wait_recv()
        mine = chunk(h, 0)
        for p in (0, 1):
            place = rows(mine + p * 128, 128)
            gp[place, :] = gp[place, :] + (rs1[h, 0, p] + rs1[h, 1, p])
        for i, d in enumerate((2, 1, 3)):
            place = rows(mine + ((across[h] + d) % 4) * SMALL, SMALL)
            send(gp.at[place, :], rs2.at[h, i], rs2_sem.at[h, 0], rs2_sem.at[h, 1], cross(h, d))
    fence()
    gg_all.wait_recv()
    half_gram = gram.at[pl.ds(c * 16, 16)]
    core_gram = send(half_gram, half_gram, cg_sem.at[0], cg_sem.at[1], at(dc=1))
    drains.append(core_gram)
    r_id = lax.broadcasted_iota(jnp.int32, (RANK, RANK), 0)
    c_id = lax.broadcasted_iota(jnp.int32, (RANK, RANK), 1)
    m[:, RANK:] = jnp.where(r_id == c_id, 1.0, 0.0).astype(F32)
    fence()
    core_gram.wait_recv()
    m[:, :RANK] = gram[...].reshape(RANK, RANK)
    fence()
    inv0 = inverse_block(m, 0)
    fence()
    ag1_all = []
    for h in both_h:
        rs2_all = group(rs2.at[h], rs2_sem.at[h, 0], rs2_sem.at[h, 1])
        rs2_all.wait_recv()
        place = rows(chunk(h, 0) + across[h] * SMALL, SMALL)
        raw[place, :] = (gp[place, :] + rs2[h, 0]) + (rs2[h, 1] + rs2[h, 2])
        for d in (2, 1, 3):
            send(raw.at[place, :], raw.at[place, :], ag1_sem.at[h, 0], ag1_sem.at[h, 1], cross(h, d))
        ag1_all.append(group(rs2.at[h], ag1_sem.at[h, 0], ag1_sem.at[h, 1]))
        drains += [rs2_all, ag1_all[h]]
    fence()
    factor_block(m, 0, inv0)
    fence()
    inv1 = inverse_block(m, 1)
    fence()
    factor_block(m, 1, inv1)
    ag2 = {}

    def gather(h, d, n, start):
        piece = raw.at[rows(start, 128), :]
        ag2[h, d, n] = send(piece, piece, ag2_send.at[n], ag2_sem.at[h, (1 - d) // 2, n], step(h, d))

    def gather_round(n):
        return group(raw.at[0:512], ag2_send.at[n], ag2_sem.at[0, 0, n])

    def first_round():
        fence()
        for cp in ag1_all:
            cp.wait_recv()
        for h in both_h:
            gather(h, 1, 0, chunk(h, 0))
            gather(h, -1, 0, chunk(h, 0) + 128)
        fence()

    def second_round():
        fence()
        for h in both_h:
            gather(h, 1, 1, chunk(h, 0) + 128)
            gather(h, -1, 1, chunk(h, 0))
        fence()

    fence()
    inv2 = inverse_block(m, 2, first_round)
    fence()
    factor_block(m, 2, inv2)
    fence()
    inv3 = inverse_block(m, 3, second_round)
    fence()
    factor_block(m, 3, inv3)

    fence()
    upper = m[:, RANK:].T
    inv = split(upper)
    groups = [
        [(chunk(h, 0), BIG) for h in both_h],
        [(start, 128) for h in both_h for start in (chunk(h, -1), chunk(h, 1) + 128)],
        [(start, 128) for h in both_h for start in (chunk(h, -1) + 128, chunk(h, 1))],
        [(start, 128) for h in both_h for start in (chunk(h, 2), chunk(h, 2) + 128)],
    ]

    def finish(g):
        pieces = jnp.concatenate([raw[rows(start, size), :] for start, size in groups[g]], axis=0)
        r = dot3(split(pieces), inv, ((1,), (0,)))
        done = 0
        for start, size in groups[g]:
            mine = rows(c * HALF + start, size)
            right[mine, :] = r[done : done + size]
            send(right.at[mine, :], right.at[mine, :], core_sem.at[g, 0], core_sem.at[g, 1], at(dc=1))
            done += size
        return r

    own = finish(0)
    for h in both_h:
        part = own[h * BIG : (h + 1) * BIG]
        sq_own[h : h + 1, :] = jnp.sum(part * part, axis=0, keepdims=True)
    for i, (dz, dc) in enumerate(COLUMN):
        send(sq_own.at[0:2], sq_in.at[i, 0:2], sq_sem.at[0], sq_sem.at[1], at(dz=dz, dc=dc))
    sq_all = group(sq_in.at[:, 0:2], sq_sem.at[0], sq_sem.at[1])
    drains.append(sq_all)
    fence()
    for h in both_h:
        ag2[h, 1, 0].wait_recv()
        gather(h, 1, 2, chunk(h, -1))
        ag2[h, -1, 0].wait_recv()
        gather(h, -1, 2, chunk(h, 1) + 128)
    drains += [gather_round(n) for n in range(3)]
    fence()
    finish(1)
    basis[...] = dot6(left[0], upper, ((1,), (0,)))
    fence()
    for h in both_h:
        ag2[h, 1, 1].wait_recv()
        ag2[h, -1, 1].wait_recv()
    fence()
    finish(2)
    fence()
    sq_all.wait_recv()
    total = sq_own[0:2, :]
    for i in range(len(COLUMN)):
        total = total + sq_in[i, 0:2, :]
    fence()
    for h in both_h:
        sq_sum[h, 0:1, :] = total[h : h + 1, :]
        for i, d in enumerate((2, 1, 3)):
            send(sq_sum.at[h, 0:1], sq_end.at[h * 3 + i, 0:1], sqe_sem.at[0], sqe_sem.at[1], step(h, d))
    sqe_all = group(sq_end.at[:, 0:1], sqe_sem.at[0], sqe_sem.at[1])
    drains.append(sqe_all)
    fence()
    for h in both_h:
        ag2[h, 1, 2].wait_recv()
        ag2[h, -1, 2].wait_recv()
    fence()
    finish(3)
    fence()
    for g in range(4):
        core_all = group(right.at[0:512], core_sem.at[g, 0], core_sem.at[g, 1])
        drains.append(core_all)
        core_all.wait_recv()
    fence()
    sqe_all.wait_recv()
    total = sq_sum[0, 0:1, :] + sq_sum[1, 0:1, :]
    for i in range(6):
        total = total + sq_end[i, 0:1, :]
    norm[...] = jnp.broadcast_to(lax.rsqrt(total + 1e-06), (8, RANK))
    fence()
    for cp in drains:
        cp.wait_send()
    w_cp.wait()


def reduce_call(mom, grad, fac, w):
    vmem = pltpu.VMEM
    dma = pltpu.SemaphoreType.DMA
    return pl.pallas_call(
        reduce_kernel,
        out_shape=(
            jax.ShapeDtypeStruct((COLS, RANK), F32),
            jax.ShapeDtypeStruct((ROWS, RANK), F32),
            jax.ShapeDtypeStruct((8, RANK), F32),
            jax.ShapeDtypeStruct((ROWS, COLS), F32),
            jax.ShapeDtypeStruct((ROWS, COLS), F32),
        ),
        in_specs=[pl.BlockSpec(memory_space=pltpu.HBM)] * 4,
        out_specs=[pl.BlockSpec(memory_space=vmem)] * 5,
        scratch_shapes=[
            vmem((ROWS, COLS), BF16),
            vmem((COLS, RANK), F32),
            vmem((ROWS, HALF), F32),
            vmem((2, HALF, RANK), BF16),
            vmem((NZ, ROWS, RANK), F32),
            vmem((2, ROWS, RANK), F32),
            vmem((128, RANK), F32),
            vmem((len(CHIPS), 8, RANK), F32),
            vmem((8, RANK), F32),
            vmem((32, 8, RANK), F32),
            vmem((RANK, 2 * RANK), F32),
            vmem((HALF, RANK), F32),
            vmem((2, 2, 128, RANK), F32),
            vmem((2, 2, 2, 128, RANK), F32),
            vmem((2, 3, SMALL, RANK), F32),
            vmem((HALF, RANK), F32),
            vmem((8, RANK), F32),
            vmem((len(COLUMN), 8, RANK), F32),
            vmem((2, 8, RANK), F32),
            vmem((6, 8, RANK), F32),
            dma((4, 3)),
            dma((2,)),
            dma((2,)),
            dma((2,)),
            dma((2,)),
            dma((2,)),
            dma((2,)),
            dma((2, 2)),
            dma((3,)),
            dma((2,)),
            dma((2, 2)),
            dma((2, 2)),
            dma((3,)),
            dma((2, 2, 3)),
            dma((4, 2)),
            dma((2,)),
            dma((2,)),
            dma((1,)),
        ],
        compiler_params=pltpu.CompilerParams(
            collective_id=0, has_side_effects=True, vmem_limit_bytes=32 * 2**20
        ),
    )(mom, grad, fac, w)


def update_kernel(
    scal, w, b, right, basis, norm, new_w_out, new_mom_out, new_fac_out, new_w, new_mom, new_fac, sem
):
    decay, rate = scal[0], scal[1]
    s = norm[0:1, :]
    q = basis[...]
    scale = rate * jnp.sqrt(jnp.float32(4096 * 16384 / RANK))
    stacked = split(jnp.concatenate([q * (1.0 - decay), q * (s * scale)], axis=0))
    wide = 512
    for i in range(COLS // wide):
        at = pl.ds(i * wide, wide)
        r = right[at, :]
        new_fac[at, :] = r * s
        pltpu.make_async_copy(new_fac.at[at, :], new_fac_out.at[at, :], sem.at[2]).start()
        d = dot3(stacked, split(r), ((1,), (1,)))
        new_mom[:, at] = b[:, at] - d[:ROWS]
        pltpu.make_async_copy(new_mom.at[:, at], new_mom_out.at[:, at], sem.at[1]).start()
        new_w[:, at] = w[:, at] - d[ROWS:]
        pltpu.make_async_copy(new_w.at[:, at], new_w_out.at[:, at], sem.at[0]).start()
    pltpu.make_async_copy(new_w, new_w_out, sem.at[0]).wait()
    pltpu.make_async_copy(new_mom, new_mom_out, sem.at[1]).wait()
    pltpu.make_async_copy(new_fac, new_fac_out, sem.at[2]).wait()


def update_call(scal, w, b, right, basis, norm):
    here = pl.BlockSpec(memory_space=pltpu.VMEM)
    outs = [(ROWS, COLS), (ROWS, COLS), (COLS, RANK)]
    return pl.pallas_call(
        update_kernel,
        out_shape=[jax.ShapeDtypeStruct(shape, F32) for shape in outs],
        in_specs=[pl.BlockSpec(memory_space=pltpu.SMEM)] + [here] * 5,
        out_specs=[pl.BlockSpec(memory_space=pl.ANY)] * 3,
        scratch_shapes=[pltpu.VMEM(shape, F32) for shape in outs] + [pltpu.SemaphoreType.DMA((3,))],
        compiler_params=pltpu.CompilerParams(vmem_limit_bytes=24 * 2**20),
    )(scal, w, b, right, basis, norm)


def body(weight, momentum, gradient, factor, decay, rate):
    keep = [pltpu.with_memory_space_constraint(a, pltpu.HBM) for a in (momentum, gradient, factor, weight)]
    right, basis, norm, b, w = reduce_call(*keep)
    scal = jnp.stack([decay, rate])
    return tuple(update_call(scal, w, b, right, basis, norm))


def solution(mesh):
    placed = (P("fsdp", "tp"), P("fsdp", "tp"), P("fsdp", "tp"), P("tp", None), P(), P())
    return jax.shard_map(
        body,
        mesh=mesh,
        in_specs=placed,
        out_specs=(P("fsdp", "tp"), P("fsdp", "tp"), P("tp", None)),
        check_vma=False,
    )
```

```python
import jax
import jax.numpy as jnp
from jax import lax
from jax.experimental import pallas as pl
from jax.experimental.pallas import tpu as pltpu
from jax.sharding import PartitionSpec as P

F32 = jnp.float32
BF16 = jnp.bfloat16
HIGH = lax.Precision.HIGHEST
MESH = pl.DeviceIdType.MESH
NX = NY = NZ = 4
ROWS, COLS, RANK = 128, 4096, 256
HALF = COLS // 2
QUARTER = HALF // 2
BIG = QUARTER // 4
SMALL = BIG // 4
CHIPS = [(dx, dy) for dx in range(NX) for dy in range(NY) if dx or dy]
RING = (1, 3, 2)
COLUMN = [(dz, dc) for dz in range(NZ) for dc in range(2) if dz or dc]


def split(x):
    hi = x.astype(BF16)
    return hi, (x - hi.astype(F32)).astype(BF16)


def dot3(a, b, dims):
    (ah, al), (bh, bl) = a, b

    def one(p, q):
        return lax.dot_general(p, q, (dims, ((), ())), preferred_element_type=F32)

    if dims[0] == (1,):
        n = ah.shape[0]
        both = one(jnp.concatenate([ah, al], axis=0), bh)
        return both[:n] + (both[n:] + one(ah, bl))
    return one(ah, bh) + (one(ah, bl) + one(al, bh))


def dot6(a, b, dims):
    return lax.dot_general(a, b, (dims, ((), ())), precision=HIGH, preferred_element_type=F32)


def row_of(t, s):
    return jnp.broadcast_to(t[s : s + 1, :], (8, 128))


def lane_of(t, l):
    return jnp.broadcast_to(t[:, l : l + 1], (8, 128))


def eliminate(d, between=None):
    nb, nt = 64, 8
    lane = lax.broadcasted_iota(jnp.int32, (8, 128), 1)
    sub = lax.broadcasted_iota(jnp.int32, (8, 128), 0)
    w = []
    for i in range(nt):
        tile = jnp.concatenate([d[8 * i : 8 * i + 8, :], jnp.zeros((8, 128 - nb), F32)], axis=1)
        w.append(jnp.where(lane == nb + 8 * i + sub, 1.0, tile))
    out = []
    for k in range(nt):
        if k == nt // 2 and between is not None:
            between()
        tile = w[k]
        cs = [lane_of(tile, 8 * k + j) for j in range(8)]
        others = [[lane_of(w[i], 8 * k + j) for j in range(8)] for i in range(k + 1, nt)]
        v = tile
        for p in range(8):
            piv = row_of(cs[p], p)
            inv = 1.0 / piv
            row = row_of(tile, p)
            mine = sub == p
            v = jnp.where(mine, row * lax.rsqrt(piv), v)
            rn = row * inv
            cz = jnp.where(mine, 0.0, cs[p])
            tile = jnp.where(mine, rn, tile) - cz * rn
            for j in range(p + 1, 8):
                rj = row_of(cs[j], p) * inv
                cs[j] = jnp.where(mine, rj, cs[j]) - cz * rj
        out.append(v)
        if k + 1 < nt:
            ts = [row_of(tile, p) for p in range(8)]
            for i in range(k + 1, nt):
                acc = [others[i - k - 1][p] * ts[p] for p in range(8)]
                while len(acc) > 1:
                    acc = [acc[q] + acc[q + 1] for q in range(0, len(acc), 2)]
                w[i] = w[i] - acc[0]
    return jnp.concatenate([o[:, nb : 2 * nb] for o in out], axis=0)


def inverse_block(m, k, between=None):
    return eliminate(m[64 * k : 64 * k + 64, 64 * k : 64 * k + 64], between)


def factor_block(m, k, inv):
    lo, hi = 64 * k, 64 * k + 64
    v = dot6(inv, m[lo:hi, :], ((1,), (0,)))
    m[lo:hi, :] = v
    if hi < RANK:
        ut = v[:, :RANK].T[hi:, :]
        m[hi:, :] -= dot6(ut, v, ((1,), (0,)))


def reduce_kernel(
    mom_hbm, grad_hbm, fac_hbm, w_hbm, right, basis, norm, mom, w,
    grad, fac, peer_b, turned, zbuf, left, gsend, grecv, gown, gram, m, gp, fwd, rs1, rs2, raw, sq_own, sq_in, sq_sum, sq_end,
    load_sem, b_sem, z_sem, l_sem, g_sem, gg_sem, cg_sem, fwd_sem, rs1_send, rs1_sem, rs2_sem, ag1_sem, ag2_send, ag2_sem,
    core_sem, sq_sem, sqe_sem, w_sem,
):
    f = lax.axis_index("fsdp")
    z = lax.axis_index("tp")
    y, x, c = f // 8, (f // 2) % 4, f % 2

    def fence():
        @pl.when(z < 0)
        def _():
            gown[...] = gown[...] + 1.0

    def at(dx=0, dy=0, dc=0, dz=0):
        return ((((y + dy) % 4) * 4 + (x + dx) % 4) * 2 + (c + dc) % 2, (z + dz) % 4)

    def copy(src, dst, send_sem, recv_sem, where):
        return pltpu.make_async_remote_copy(
            src, dst, send_sem, recv_sem, device_id=where, device_id_type=MESH
        )

    drains = []

    def send(src, dst, send_sem, recv_sem, where):
        cp = copy(src, dst, send_sem, recv_sem, where)
        cp.start()
        return cp

    def group(ref, send_sem, recv_sem):
        return copy(ref, ref, send_sem, recv_sem, at(dc=1))

    def write(src, dst, sem):
        cp = pltpu.make_async_copy(src, dst, sem)
        cp.start()
        return cp

    def rows(start, size):
        return pl.ds(pl.multiple_of(start, size), size)

    fence()
    barrier = pltpu.get_barrier_semaphore()
    partners = [at(dx, dy) for dx, dy in CHIPS] + [at(dz=dz, dc=dc) for dz, dc in COLUMN]
    for partner in partners:
        pl.semaphore_signal(barrier, inc=1, device_id=partner, device_id_type=MESH)
    blocks, ahead = 4, 4
    wide = COLS // blocks

    def load(q):
        cols = pl.ds(q * wide, wide)
        trio = [
            pltpu.make_async_copy(mom_hbm.at[:, cols], mom.at[:, cols], load_sem.at[q, 0]),
            pltpu.make_async_copy(grad_hbm.at[:, cols], grad.at[:, cols], load_sem.at[q, 1]),
            pltpu.make_async_copy(fac_hbm.at[cols, :], fac.at[cols, :], load_sem.at[q, 2]),
        ]
        for cp in trio:
            cp.start()
        return trio

    loads = [load(q) for q in range(ahead)]

    fence()
    part = None
    for q in range(blocks):
        for cp in loads[q]:
            cp.wait()
        if q + ahead < blocks:
            loads.append(load(q + ahead))
        cols = pl.ds(q * wide, wide)
        b = mom[:, cols] + grad[:, cols].astype(F32)
        mom[:, cols] = b
        p = dot3(split(b), split(fac[cols, :]), ((1,), (0,)))
        part = p if part is None else part + p
    zbuf[z] = part
    fence()
    pl.semaphore_wait(barrier, len(partners))
    fence()
    for dz in RING:
        send(zbuf.at[z], zbuf.at[z], z_sem.at[0], z_sem.at[1], at(dz=dz))
    z_all = group(zbuf.at[0:3], z_sem.at[0], z_sem.at[1])
    b_cp = send(mom.at[:, rows((1 - c) * HALF, HALF)], peer_b, b_sem.at[0], b_sem.at[1], at(dc=1))
    drains += [z_all, b_cp]
    w_cp = write(w_hbm, w, w_sem.at[0])
    fence()
    b_cp.wait_recv()
    for i in range(HALF // BIG):
        part = jnp.concatenate([mom[:, rows(c * HALF + i * BIG, BIG)], peer_b[:, i * BIG : (i + 1) * BIG]], axis=0)
        hi, lo = split(part.T)
        turned[0, i * BIG : (i + 1) * BIG, :] = hi
        turned[1, i * BIG : (i + 1) * BIG, :] = lo
    fence()
    z_all.wait_recv()
    left[0] = (zbuf[0] + zbuf[1]) + (zbuf[2] + zbuf[3])
    l_cp = send(left.at[0], left.at[1], l_sem.at[0], l_sem.at[1], at(dc=1))
    drains.append(l_cp)
    fence()
    l_cp.wait_recv()
    both = left[...].reshape(2 * ROWS, RANK)

    fence()
    lh, ll = split(both)

    def product(start):
        place = rows(start, BIG)
        gp[place, :] = dot3((turned[0, place, :], turned[1, place, :]), (lh, ll), ((1,), (0,)))

    def step(h, d):
        return at(dx=d) if h == 0 else at(dy=d)

    def cross(h, d):
        return at(dy=d) if h == 0 else at(dx=d)

    along, across = (x, y), (y, x)
    both_h = (0, 1)

    def chunk(h, d):
        return h * QUARTER + ((along[h] + d) % 4) * BIG

    fwd_cps = {}
    for h in both_h:
        far = chunk(h, 2)
        product(far)
        for n, d in ((0, 1), (1, -1)):
            place = rows(far + n * 128, 128)
            fwd_cps[h, n] = send(gp.at[place, :], fwd.at[h, n], rs1_send.at[0], fwd_sem.at[h, n], step(h, d))
    fence()
    mine = left[:, :, rows(c * 128, 128)].reshape(2 * ROWS, 128)
    gsend[...] = dot6(mine, both, ((0,), (0,)))
    fence()
    chip = y * 4 + x
    for i, (dx, dy) in enumerate(CHIPS):
        other = ((y + dy) % 4) * 4 + (x + dx) % 4
        send(gsend.at[rows(other * 8, 8), :], grecv.at[i], g_sem.at[0], g_sem.at[1], at(dx, dy))
    g_all = group(grecv, g_sem.at[0], g_sem.at[1])

    fence()
    for h in both_h:
        product(chunk(h, 1))
        product(chunk(h, -1))
    for h in both_h:
        product(chunk(h, 0))
    fence()
    for h in both_h:
        for n, d in ((1, 1), (0, -1)):
            place = rows(chunk(h, d) + n * 128, 128)
            send(gp.at[place, :], rs1.at[h, 1 - n, n], rs1_send.at[1], rs1_sem.at[h], step(h, d))
    drains.append(group(fwd, rs1_send.at[0], fwd_sem.at[0, 0]))
    fence()
    for h in both_h:
        for n, d in ((0, 1), (1, -1)):
            place = rows(chunk(h, d) + n * 128, 128)
            fwd_cps[h, n].wait_recv()
            gp[place, :] = gp[place, :] + fwd[h, n]
            send(gp.at[place, :], rs1.at[h, n, n], rs1_send.at[2], rs1_sem.at[h], step(h, d))
    fence()
    g_all.wait_recv()
    total = gsend[rows(chip * 8, 8), :]
    for i in range(len(CHIPS)):
        total = total + grecv[i]
    fence()
    gown[...] = total
    gram[c * 16 + chip] = total
    for dx, dy in CHIPS:
        send(gown, gram.at[c * 16 + chip], gg_sem.at[0], gg_sem.at[1], at(dx, dy))
    gg_all = group(grecv, gg_sem.at[0], gg_sem.at[1])
    drains += [g_all, gg_all]

    fence()
    for h in both_h:
        rs1_all = group(rs1.at[h], rs1_send.at[1 + h], rs1_sem.at[h])
        drains.append(rs1_all)
        rs1_all.wait_recv()
        mine = chunk(h, 0)
        for p in (0, 1):
            place = rows(mine + p * 128, 128)
            gp[place, :] = gp[place, :] + (rs1[h, 0, p] + rs1[h, 1, p])
        for i, d in enumerate((2, 1, 3)):
            place = rows(mine + ((across[h] + d) % 4) * SMALL, SMALL)
            send(gp.at[place, :], rs2.at[h, i], rs2_sem.at[h, 0], rs2_sem.at[h, 1], cross(h, d))
    fence()
    gg_all.wait_recv()
    half_gram = gram.at[pl.ds(c * 16, 16)]
    core_gram = send(half_gram, half_gram, cg_sem.at[0], cg_sem.at[1], at(dc=1))
    drains.append(core_gram)
    r_id = lax.broadcasted_iota(jnp.int32, (RANK, RANK), 0)
    c_id = lax.broadcasted_iota(jnp.int32, (RANK, RANK), 1)
    m[:, RANK:] = jnp.where(r_id == c_id, 1.0, 0.0).astype(F32)
    fence()
    core_gram.wait_recv()
    m[:, :RANK] = gram[...].reshape(RANK, RANK)
    fence()
    inv0 = inverse_block(m, 0)
    fence()
    ag1_all = []
    for h in both_h:
        rs2_all = group(rs2.at[h], rs2_sem.at[h, 0], rs2_sem.at[h, 1])
        rs2_all.wait_recv()
        place = rows(chunk(h, 0) + across[h] * SMALL, SMALL)
        raw[place, :] = (gp[place, :] + rs2[h, 0]) + (rs2[h, 1] + rs2[h, 2])
        for d in (2, 1, 3):
            send(raw.at[place, :], raw.at[place, :], ag1_sem.at[h, 0], ag1_sem.at[h, 1], cross(h, d))
        ag1_all.append(group(rs2.at[h], ag1_sem.at[h, 0], ag1_sem.at[h, 1]))
        drains += [rs2_all, ag1_all[h]]
    fence()
    factor_block(m, 0, inv0)
    fence()
    inv1 = inverse_block(m, 1)
    fence()
    factor_block(m, 1, inv1)
    ag2 = {}

    def gather(h, d, n, start):
        piece = raw.at[rows(start, 128), :]
        ag2[h, d, n] = send(piece, piece, ag2_send.at[n], ag2_sem.at[h, (1 - d) // 2, n], step(h, d))

    def gather_round(n):
        return group(raw.at[0:512], ag2_send.at[n], ag2_sem.at[0, 0, n])

    def first_round():
        fence()
        for cp in ag1_all:
            cp.wait_recv()
        for h in both_h:
            gather(h, 1, 0, chunk(h, 0))
            gather(h, -1, 0, chunk(h, 0) + 128)
        fence()

    def second_round():
        fence()
        for h in both_h:
            gather(h, 1, 1, chunk(h, 0) + 128)
            gather(h, -1, 1, chunk(h, 0))
        fence()

    fence()
    inv2 = inverse_block(m, 2, first_round)
    fence()
    factor_block(m, 2, inv2)
    fence()
    inv3 = inverse_block(m, 3, second_round)
    fence()
    factor_block(m, 3, inv3)

    fence()
    upper = m[:, RANK:].T
    inv = split(upper)
    groups = [
        [(chunk(h, 0), BIG) for h in both_h],
        [(start, 128) for h in both_h for start in (chunk(h, -1), chunk(h, 1) + 128)],
        [(start, 128) for h in both_h for start in (chunk(h, -1) + 128, chunk(h, 1))],
        [(chunk(0, 2), 128), (chunk(0, 2) + 128, 128)],
        [(chunk(1, 2), 128), (chunk(1, 2) + 128, 128)],
    ]

    def finish(g):
        pieces = jnp.concatenate([raw[rows(start, size), :] for start, size in groups[g]], axis=0)
        r = dot3(split(pieces), inv, ((1,), (0,)))
        done = 0
        for start, size in groups[g]:
            mine = rows(c * HALF + start, size)
            right[mine, :] = r[done : done + size]
            send(right.at[mine, :], right.at[mine, :], core_sem.at[g, 0], core_sem.at[g, 1], at(dc=1))
            done += size
        return r

    own = finish(0)
    for h in both_h:
        part = own[h * BIG : (h + 1) * BIG]
        sq_own[h : h + 1, :] = jnp.sum(part * part, axis=0, keepdims=True)
    for i, (dz, dc) in enumerate(COLUMN):
        send(sq_own.at[0:2], sq_in.at[i, 0:2], sq_sem.at[0], sq_sem.at[1], at(dz=dz, dc=dc))
    sq_all = group(sq_in.at[:, 0:2], sq_sem.at[0], sq_sem.at[1])
    drains.append(sq_all)
    fence()
    for h in both_h:
        ag2[h, 1, 0].wait_recv()
        gather(h, 1, 2, chunk(h, -1))
        ag2[h, -1, 0].wait_recv()
        gather(h, -1, 2, chunk(h, 1) + 128)
    drains += [gather_round(n) for n in range(3)]
    fence()
    finish(1)
    basis[...] = dot6(left[0], upper, ((1,), (0,)))
    fence()
    for h in both_h:
        ag2[h, 1, 1].wait_recv()
        ag2[h, -1, 1].wait_recv()
    fence()
    finish(2)
    fence()
    sq_all.wait_recv()
    total = sq_own[0:2, :]
    for i in range(len(COLUMN)):
        total = total + sq_in[i, 0:2, :]
    fence()
    for h in both_h:
        sq_sum[h, 0:1, :] = total[h : h + 1, :]
        for i, d in enumerate((2, 1, 3)):
            send(sq_sum.at[h, 0:1], sq_end.at[h * 3 + i, 0:1], sqe_sem.at[0], sqe_sem.at[1], step(h, d))
    sqe_all = group(sq_end.at[:, 0:1], sqe_sem.at[0], sqe_sem.at[1])
    drains.append(sqe_all)
    fence()
    for h in both_h:
        ag2[h, 1, 2].wait_recv()
        ag2[h, -1, 2].wait_recv()
        fence()
        finish(3 + h)
        fence()
    for g, pieces in enumerate(groups):
        core_all = group(right.at[0 : sum(size for _, size in pieces)], core_sem.at[g, 0], core_sem.at[g, 1])
        drains.append(core_all)
        core_all.wait_recv()
    fence()
    sqe_all.wait_recv()
    total = sq_sum[0, 0:1, :] + sq_sum[1, 0:1, :]
    for i in range(6):
        total = total + sq_end[i, 0:1, :]
    norm[...] = jnp.broadcast_to(lax.rsqrt(total + 1e-06), (8, RANK))
    fence()
    for cp in drains:
        cp.wait_send()
    w_cp.wait()


def reduce_call(mom, grad, fac, w):
    vmem = pltpu.VMEM
    dma = pltpu.SemaphoreType.DMA
    return pl.pallas_call(
        reduce_kernel,
        out_shape=(
            jax.ShapeDtypeStruct((COLS, RANK), F32),
            jax.ShapeDtypeStruct((ROWS, RANK), F32),
            jax.ShapeDtypeStruct((8, RANK), F32),
            jax.ShapeDtypeStruct((ROWS, COLS), F32),
            jax.ShapeDtypeStruct((ROWS, COLS), F32),
        ),
        in_specs=[pl.BlockSpec(memory_space=pltpu.HBM)] * 4,
        out_specs=[pl.BlockSpec(memory_space=vmem)] * 5,
        scratch_shapes=[
            vmem((ROWS, COLS), BF16),
            vmem((COLS, RANK), F32),
            vmem((ROWS, HALF), F32),
            vmem((2, HALF, RANK), BF16),
            vmem((NZ, ROWS, RANK), F32),
            vmem((2, ROWS, RANK), F32),
            vmem((128, RANK), F32),
            vmem((len(CHIPS), 8, RANK), F32),
            vmem((8, RANK), F32),
            vmem((32, 8, RANK), F32),
            vmem((RANK, 2 * RANK), F32),
            vmem((HALF, RANK), F32),
            vmem((2, 2, 128, RANK), F32),
            vmem((2, 2, 2, 128, RANK), F32),
            vmem((2, 3, SMALL, RANK), F32),
            vmem((HALF, RANK), F32),
            vmem((8, RANK), F32),
            vmem((len(COLUMN), 8, RANK), F32),
            vmem((2, 8, RANK), F32),
            vmem((6, 8, RANK), F32),
            dma((4, 3)),
            dma((2,)),
            dma((2,)),
            dma((2,)),
            dma((2,)),
            dma((2,)),
            dma((2,)),
            dma((2, 2)),
            dma((3,)),
            dma((2,)),
            dma((2, 2)),
            dma((2, 2)),
            dma((3,)),
            dma((2, 2, 3)),
            dma((5, 2)),
            dma((2,)),
            dma((2,)),
            dma((1,)),
        ],
        compiler_params=pltpu.CompilerParams(
            collective_id=0, has_side_effects=True, vmem_limit_bytes=32 * 2**20
        ),
    )(mom, grad, fac, w)


def update_kernel(
    scal, w, b, right, basis, norm, new_w_out, new_mom_out, new_fac_out, new_w, new_mom, new_fac, sem
):
    decay, rate = scal[0], scal[1]
    s = norm[0:1, :]
    q = basis[...]
    scale = rate * jnp.sqrt(jnp.float32(4096 * 16384 / RANK))
    stacked = split(jnp.concatenate([q * (1.0 - decay), q * (s * scale)], axis=0))
    wide = 512
    for i in range(COLS // wide):
        at = pl.ds(i * wide, wide)
        r = right[at, :]
        new_fac[at, :] = r * s
        pltpu.make_async_copy(new_fac.at[at, :], new_fac_out.at[at, :], sem.at[2]).start()
        d = dot3(stacked, split(r), ((1,), (1,)))
        new_mom[:, at] = b[:, at] - d[:ROWS]
        pltpu.make_async_copy(new_mom.at[:, at], new_mom_out.at[:, at], sem.at[1]).start()
        new_w[:, at] = w[:, at] - d[ROWS:]
        pltpu.make_async_copy(new_w.at[:, at], new_w_out.at[:, at], sem.at[0]).start()
    pltpu.make_async_copy(new_w, new_w_out, sem.at[0]).wait()
    pltpu.make_async_copy(new_mom, new_mom_out, sem.at[1]).wait()
    pltpu.make_async_copy(new_fac, new_fac_out, sem.at[2]).wait()


def update_call(scal, w, b, right, basis, norm):
    here = pl.BlockSpec(memory_space=pltpu.VMEM)
    outs = [(ROWS, COLS), (ROWS, COLS), (COLS, RANK)]
    return pl.pallas_call(
        update_kernel,
        out_shape=[jax.ShapeDtypeStruct(shape, F32) for shape in outs],
        in_specs=[pl.BlockSpec(memory_space=pltpu.SMEM)] + [here] * 5,
        out_specs=[pl.BlockSpec(memory_space=pl.ANY)] * 3,
        scratch_shapes=[pltpu.VMEM(shape, F32) for shape in outs] + [pltpu.SemaphoreType.DMA((3,))],
        compiler_params=pltpu.CompilerParams(vmem_limit_bytes=24 * 2**20),
    )(scal, w, b, right, basis, norm)


def body(weight, momentum, gradient, factor, decay, rate):
    keep = [pltpu.with_memory_space_constraint(a, pltpu.HBM) for a in (momentum, gradient, factor, weight)]
    right, basis, norm, b, w = reduce_call(*keep)
    scal = jnp.stack([decay, rate])
    return tuple(update_call(scal, w, b, right, basis, norm))


def solution(mesh):
    placed = (P("fsdp", "tp"), P("fsdp", "tp"), P("fsdp", "tp"), P("tp", None), P(), P())
    return jax.shard_map(
        body,
        mesh=mesh,
        in_specs=placed,
        out_specs=(P("fsdp", "tp"), P("fsdp", "tp"), P("tp", None)),
        check_vma=False,
    )
```

```python
import jax
import jax.numpy as jnp
from jax import lax
from jax.experimental import pallas as pl
from jax.experimental.pallas import tpu as pltpu
from jax.sharding import PartitionSpec as P

F32 = jnp.float32
BF16 = jnp.bfloat16
HIGH = lax.Precision.HIGHEST
MESH = pl.DeviceIdType.MESH
NX = NY = NZ = 4
ROWS, COLS, RANK = 128, 4096, 256
HALF = COLS // 2
QUARTER = HALF // 2
BIG = QUARTER // 4
SMALL = BIG // 4
CHIPS = [(dx, dy) for dx in range(NX) for dy in range(NY) if dx or dy]
RING = (1, 3, 2)
ONWARD = {1: ((1, 0, 64), (2, 0, 32)), -1: ((3, 0, 64), (2, 32, 32))}
ROUNDS = (256, 384, 384, 128, 384)
COLUMN = [(dz, dc) for dz in range(NZ) for dc in range(2) if dz or dc]


def split(x):
    hi = x.astype(BF16)
    return hi, (x - hi.astype(F32)).astype(BF16)


def dot3(a, b, dims):
    (ah, al), (bh, bl) = a, b

    def one(p, q):
        return lax.dot_general(p, q, (dims, ((), ())), preferred_element_type=F32)

    if dims[0] == (1,):
        n = ah.shape[0]
        both = one(jnp.concatenate([ah, al], axis=0), bh)
        return both[:n] + (both[n:] + one(ah, bl))
    return one(ah, bh) + (one(ah, bl) + one(al, bh))


def dot6(a, b, dims):
    return lax.dot_general(a, b, (dims, ((), ())), precision=HIGH, preferred_element_type=F32)


def row_of(t, s):
    return jnp.broadcast_to(t[s : s + 1, :], (8, 128))


def lane_of(t, l):
    return jnp.broadcast_to(t[:, l : l + 1], (8, 128))


def eliminate(d, between=None):
    nb, nt = 64, 8
    lane = lax.broadcasted_iota(jnp.int32, (8, 128), 1)
    sub = lax.broadcasted_iota(jnp.int32, (8, 128), 0)
    w = []
    for i in range(nt):
        tile = jnp.concatenate([d[8 * i : 8 * i + 8, :], jnp.zeros((8, 128 - nb), F32)], axis=1)
        w.append(jnp.where(lane == nb + 8 * i + sub, 1.0, tile))
    out = []
    for k in range(nt):
        if k == nt // 2 and between is not None:
            between()
        tile = w[k]
        cs = [lane_of(tile, 8 * k + j) for j in range(8)]
        others = [[lane_of(w[i], 8 * k + j) for j in range(8)] for i in range(k + 1, nt)]
        v = tile
        for p in range(8):
            piv = row_of(cs[p], p)
            inv = 1.0 / piv
            row = row_of(tile, p)
            mine = sub == p
            v = jnp.where(mine, row * lax.rsqrt(piv), v)
            rn = row * inv
            cz = jnp.where(mine, 0.0, cs[p])
            tile = jnp.where(mine, rn, tile) - cz * rn
            for j in range(p + 1, 8):
                rj = row_of(cs[j], p) * inv
                cs[j] = jnp.where(mine, rj, cs[j]) - cz * rj
        out.append(v)
        if k + 1 < nt:
            ts = [row_of(tile, p) for p in range(8)]
            for i in range(k + 1, nt):
                acc = [others[i - k - 1][p] * ts[p] for p in range(8)]
                while len(acc) > 1:
                    acc = [acc[q] + acc[q + 1] for q in range(0, len(acc), 2)]
                w[i] = w[i] - acc[0]
    return jnp.concatenate([o[:, nb : 2 * nb] for o in out], axis=0)


def inverse_block(m, k, between=None):
    return eliminate(m[64 * k : 64 * k + 64, 64 * k : 64 * k + 64], between)


def factor_block(m, k, inv):
    lo, hi = 64 * k, 64 * k + 64
    v = dot6(inv, m[lo:hi, :], ((1,), (0,)))
    m[lo:hi, :] = v
    if hi < RANK:
        ut = v[:, :RANK].T[hi:, :]
        m[hi:, :] -= dot6(ut, v, ((1,), (0,)))


def reduce_kernel(
    mom_hbm, grad_hbm, fac_hbm, w_hbm, right, basis, norm, mom, w,
    grad, fac, peer_b, turned, zbuf, left, gsend, grecv, gown, gram, m, gp, fwd, rs1, rs2, raw, sq_own, sq_in, sq_sum, sq_end,
    load_sem, b_sem, z_sem, l_sem, g_sem, gg_sem, cg_sem, fwd_sem, rs1_send, rs1_sem, rs2_sem, ag1_sem, ag2_send, ag2_sem,
    core_sem, sq_sem, sqe_sem, w_sem,
):
    f = lax.axis_index("fsdp")
    z = lax.axis_index("tp")
    y, x, c = f // 8, (f // 2) % 4, f % 2

    def fence():
        @pl.when(z < 0)
        def _():
            gown[...] = gown[...] + 1.0

    def at(dx=0, dy=0, dc=0, dz=0):
        return ((((y + dy) % 4) * 4 + (x + dx) % 4) * 2 + (c + dc) % 2, (z + dz) % 4)

    def copy(src, dst, send_sem, recv_sem, where):
        return pltpu.make_async_remote_copy(
            src, dst, send_sem, recv_sem, device_id=where, device_id_type=MESH
        )

    drains = []

    def send(src, dst, send_sem, recv_sem, where):
        cp = copy(src, dst, send_sem, recv_sem, where)
        cp.start()
        return cp

    def group(ref, send_sem, recv_sem):
        return copy(ref, ref, send_sem, recv_sem, at(dc=1))

    def write(src, dst, sem):
        cp = pltpu.make_async_copy(src, dst, sem)
        cp.start()
        return cp

    def rows(start, size):
        return pl.ds(pl.multiple_of(start, size), size)

    fence()
    barrier = pltpu.get_barrier_semaphore()
    partners = [at(dx, dy) for dx, dy in CHIPS] + [at(dz=dz, dc=dc) for dz, dc in COLUMN]
    for partner in partners:
        pl.semaphore_signal(barrier, inc=1, device_id=partner, device_id_type=MESH)
    blocks, ahead = 4, 4
    wide = COLS // blocks

    def load(q):
        cols = pl.ds(q * wide, wide)
        trio = [
            pltpu.make_async_copy(mom_hbm.at[:, cols], mom.at[:, cols], load_sem.at[q, 0]),
            pltpu.make_async_copy(grad_hbm.at[:, cols], grad.at[:, cols], load_sem.at[q, 1]),
            pltpu.make_async_copy(fac_hbm.at[cols, :], fac.at[cols, :], load_sem.at[q, 2]),
        ]
        for cp in trio:
            cp.start()
        return trio

    loads = [load(q) for q in range(ahead)]

    fence()
    part = None
    for q in range(blocks):
        for cp in loads[q]:
            cp.wait()
        if q + ahead < blocks:
            loads.append(load(q + ahead))
        cols = pl.ds(q * wide, wide)
        b = mom[:, cols] + grad[:, cols].astype(F32)
        mom[:, cols] = b
        p = dot3(split(b), split(fac[cols, :]), ((1,), (0,)))
        part = p if part is None else part + p
    zbuf[z] = part
    fence()
    pl.semaphore_wait(barrier, len(partners))
    fence()
    for dz in RING:
        send(zbuf.at[z], zbuf.at[z], z_sem.at[0], z_sem.at[1], at(dz=dz))
    z_all = group(zbuf.at[0:3], z_sem.at[0], z_sem.at[1])
    b_cp = send(mom.at[:, rows((1 - c) * HALF, HALF)], peer_b, b_sem.at[0], b_sem.at[1], at(dc=1))
    drains += [z_all, b_cp]
    w_cp = write(w_hbm, w, w_sem.at[0])
    fence()
    b_cp.wait_recv()
    for i in range(HALF // BIG):
        part = jnp.concatenate([mom[:, rows(c * HALF + i * BIG, BIG)], peer_b[:, i * BIG : (i + 1) * BIG]], axis=0)
        hi, lo = split(part.T)
        turned[0, i * BIG : (i + 1) * BIG, :] = hi
        turned[1, i * BIG : (i + 1) * BIG, :] = lo
    fence()
    z_all.wait_recv()
    left[0] = (zbuf[0] + zbuf[1]) + (zbuf[2] + zbuf[3])
    l_cp = send(left.at[0], left.at[1], l_sem.at[0], l_sem.at[1], at(dc=1))
    drains.append(l_cp)
    fence()
    l_cp.wait_recv()
    both = left[...].reshape(2 * ROWS, RANK)

    fence()
    lh, ll = split(both)

    def product(start):
        place = rows(start, BIG)
        gp[place, :] = dot3((turned[0, place, :], turned[1, place, :]), (lh, ll), ((1,), (0,)))

    def step(h, d):
        return at(dx=d) if h == 0 else at(dy=d)

    def cross(h, d):
        return at(dy=d) if h == 0 else at(dx=d)

    along, across = (x, y), (y, x)
    both_h = (0, 1)

    def chunk(h, d):
        return h * QUARTER + ((along[h] + d) % 4) * BIG

    fwd_cps = {}
    for h in both_h:
        far = chunk(h, 2)
        product(far)
        for n, d in ((0, 1), (1, -1)):
            place = rows(far + n * 128, 128)
            fwd_cps[h, n] = send(gp.at[place, :], fwd.at[h, n], rs1_send.at[0], fwd_sem.at[h, n], step(h, d))
    fence()
    mine = left[:, :, rows(c * 128, 128)].reshape(2 * ROWS, 128)
    gsend[...] = dot6(mine, both, ((0,), (0,)))
    fence()
    chip = y * 4 + x
    for i, (dx, dy) in enumerate(CHIPS):
        other = ((y + dy) % 4) * 4 + (x + dx) % 4
        send(gsend.at[rows(other * 8, 8), :], grecv.at[i], g_sem.at[0], g_sem.at[1], at(dx, dy))
    g_all = group(grecv, g_sem.at[0], g_sem.at[1])

    fence()
    for h in both_h:
        product(chunk(h, 1))
        product(chunk(h, -1))
    for h in both_h:
        product(chunk(h, 0))
    fence()
    for h in both_h:
        for n, d in ((1, 1), (0, -1)):
            place = rows(chunk(h, d) + n * 128, 128)
            send(gp.at[place, :], rs1.at[h, 1 - n, n], rs1_send.at[1], rs1_sem.at[h], step(h, d))
    drains.append(group(fwd, rs1_send.at[0], fwd_sem.at[0, 0]))
    fence()
    for h in both_h:
        for n, d in ((0, 1), (1, -1)):
            place = rows(chunk(h, d) + n * 128, 128)
            fwd_cps[h, n].wait_recv()
            gp[place, :] = gp[place, :] + fwd[h, n]
            send(gp.at[place, :], rs1.at[h, n, n], rs1_send.at[2], rs1_sem.at[h], step(h, d))
    fence()
    g_all.wait_recv()
    total = gsend[rows(chip * 8, 8), :]
    for i in range(len(CHIPS)):
        total = total + grecv[i]
    fence()
    gown[...] = total
    gram[c * 16 + chip] = total
    for dx, dy in CHIPS:
        send(gown, gram.at[c * 16 + chip], gg_sem.at[0], gg_sem.at[1], at(dx, dy))
    gg_all = group(grecv, gg_sem.at[0], gg_sem.at[1])
    drains += [g_all, gg_all]

    fence()
    for h in both_h:
        rs1_all = group(rs1.at[h], rs1_send.at[1 + h], rs1_sem.at[h])
        drains.append(rs1_all)
        rs1_all.wait_recv()
        mine = chunk(h, 0)
        for p in (0, 1):
            place = rows(mine + p * 128, 128)
            gp[place, :] = gp[place, :] + (rs1[h, 0, p] + rs1[h, 1, p])
        for i, d in enumerate((2, 1, 3)):
            place = rows(mine + ((across[h] + d) % 4) * SMALL, SMALL)
            send(gp.at[place, :], rs2.at[h, i], rs2_sem.at[h, 0], rs2_sem.at[h, 1], cross(h, d))
    fence()
    gg_all.wait_recv()
    half_gram = gram.at[pl.ds(c * 16, 16)]
    core_gram = send(half_gram, half_gram, cg_sem.at[0], cg_sem.at[1], at(dc=1))
    drains.append(core_gram)
    r_id = lax.broadcasted_iota(jnp.int32, (RANK, RANK), 0)
    c_id = lax.broadcasted_iota(jnp.int32, (RANK, RANK), 1)
    m[:, RANK:] = jnp.where(r_id == c_id, 1.0, 0.0).astype(F32)
    fence()
    core_gram.wait_recv()
    m[:, :RANK] = gram[...].reshape(RANK, RANK)
    fence()
    inv0 = inverse_block(m, 0)
    fence()
    ag1_all = []
    for h in both_h:
        rs2_all = group(rs2.at[h], rs2_sem.at[h, 0], rs2_sem.at[h, 1])
        rs2_all.wait_recv()
        place = rows(chunk(h, 0) + across[h] * SMALL, SMALL)
        raw[place, :] = (gp[place, :] + rs2[h, 0]) + (rs2[h, 1] + rs2[h, 2])
        for d in (2, 1, 3):
            send(raw.at[place, :], raw.at[place, :], ag1_sem.at[h, 0], ag1_sem.at[h, 1], cross(h, d))
        ag1_all.append(group(rs2.at[h], ag1_sem.at[h, 0], ag1_sem.at[h, 1]))
        drains += [rs2_all, ag1_all[h]]
    fence()
    factor_block(m, 0, inv0)
    fence()
    inv1 = inverse_block(m, 1)
    fence()
    def gather(n, h, d, j, subs):
        for k, first, size in subs:
            start = chunk(h, j) + ((across[h] + k) % 4) * SMALL + first
            piece = raw.at[rows(start, size), :]
            send(piece, piece, ag2_send.at[n], ag2_sem.at[h, (1 - d) // 2, n], step(h, d))

    def gathered(n, h, d):
        size = ROUNDS[n] // 4
        group(raw.at[0:size], ag2_send.at[n], ag2_sem.at[h, (1 - d) // 2, n]).wait_recv()

    for h in both_h:
        for d in (1, -1):
            gather(0, h, d, 0, ((0, 0, SMALL),))
    fence()
    factor_block(m, 1, inv1)
    def first_round():
        fence()
        for cp in ag1_all:
            cp.wait_recv()
        for h in both_h:
            for d in (1, -1):
                gather(1, h, d, 0, ONWARD[d])
        fence()

    def second_round():
        fence()
        for h in both_h:
            for d in (1, -1):
                gather(2, h, d, 0, ONWARD[-d])
        for h in both_h:
            for d in (1, -1):
                gathered(0, h, d)
                gather(3, h, d, -d, ((0, 16 - 16 * d, 32),))
        fence()

    fence()
    inv2 = inverse_block(m, 2, first_round)
    fence()
    factor_block(m, 2, inv2)
    fence()
    inv3 = inverse_block(m, 3, second_round)
    fence()
    factor_block(m, 3, inv3)

    fence()
    upper = m[:, RANK:].T
    inv = split(upper)
    groups = [
        [(chunk(h, 0), BIG) for h in both_h],
        [(chunk(h, -1), BIG) for h in both_h],
        [(chunk(h, 1), BIG) for h in both_h],
        [(chunk(0, 2), BIG)],
        [(chunk(1, 2), BIG)],
    ]

    def finish(g):
        pieces = jnp.concatenate([raw[rows(start, size), :] for start, size in groups[g]], axis=0)
        r = dot3(split(pieces), inv, ((1,), (0,)))
        done = 0
        for start, size in groups[g]:
            mine = rows(c * HALF + start, size)
            right[mine, :] = r[done : done + size]
            send(right.at[mine, :], right.at[mine, :], core_sem.at[g, 0], core_sem.at[g, 1], at(dc=1))
            done += size
        return r

    own = finish(0)
    for h in both_h:
        part = own[h * BIG : (h + 1) * BIG]
        sq_own[h : h + 1, :] = jnp.sum(part * part, axis=0, keepdims=True)
    for i, (dz, dc) in enumerate(COLUMN):
        send(sq_own.at[0:2], sq_in.at[i, 0:2], sq_sem.at[0], sq_sem.at[1], at(dz=dz, dc=dc))
    sq_all = group(sq_in.at[:, 0:2], sq_sem.at[0], sq_sem.at[1])
    drains.append(sq_all)
    fence()
    for h in both_h:
        for d in (1, -1):
            gathered(1, h, d)
            gather(4, h, d, -d, ONWARD[d])
    drains += [group(raw.at[0:size], ag2_send.at[n], ag2_sem.at[0, 0, n]) for n, size in enumerate(ROUNDS)]
    fence()
    basis[...] = dot6(left[0], upper, ((1,), (0,)))
    fence()
    for h in both_h:
        gathered(2, h, 1)
        gathered(2, h, -1)
    fence()
    finish(1)
    finish(2)
    fence()
    sq_all.wait_recv()
    total = sq_own[0:2, :]
    for i in range(len(COLUMN)):
        total = total + sq_in[i, 0:2, :]
    fence()
    for h in both_h:
        sq_sum[h, 0:1, :] = total[h : h + 1, :]
        for i, d in enumerate((2, 1, 3)):
            send(sq_sum.at[h, 0:1], sq_end.at[h * 3 + i, 0:1], sqe_sem.at[0], sqe_sem.at[1], step(h, d))
    sqe_all = group(sq_end.at[:, 0:1], sqe_sem.at[0], sqe_sem.at[1])
    drains.append(sqe_all)
    fence()
    for h in both_h:
        for d in (1, -1):
            gathered(3, h, d)
            gathered(4, h, d)
        fence()
        finish(3 + h)
        fence()
    for g, pieces in enumerate(groups):
        core_all = group(right.at[0 : sum(size for _, size in pieces)], core_sem.at[g, 0], core_sem.at[g, 1])
        drains.append(core_all)
        core_all.wait_recv()
    fence()
    sqe_all.wait_recv()
    total = sq_sum[0, 0:1, :] + sq_sum[1, 0:1, :]
    for i in range(6):
        total = total + sq_end[i, 0:1, :]
    norm[...] = jnp.broadcast_to(lax.rsqrt(total + 1e-06), (8, RANK))
    fence()
    for cp in drains:
        cp.wait_send()
    w_cp.wait()


def reduce_call(mom, grad, fac, w):
    vmem = pltpu.VMEM
    dma = pltpu.SemaphoreType.DMA
    return pl.pallas_call(
        reduce_kernel,
        out_shape=(
            jax.ShapeDtypeStruct((COLS, RANK), F32),
            jax.ShapeDtypeStruct((ROWS, RANK), F32),
            jax.ShapeDtypeStruct((8, RANK), F32),
            jax.ShapeDtypeStruct((ROWS, COLS), F32),
            jax.ShapeDtypeStruct((ROWS, COLS), F32),
        ),
        in_specs=[pl.BlockSpec(memory_space=pltpu.HBM)] * 4,
        out_specs=[pl.BlockSpec(memory_space=vmem)] * 5,
        scratch_shapes=[
            vmem((ROWS, COLS), BF16),
            vmem((COLS, RANK), F32),
            vmem((ROWS, HALF), F32),
            vmem((2, HALF, RANK), BF16),
            vmem((NZ, ROWS, RANK), F32),
            vmem((2, ROWS, RANK), F32),
            vmem((128, RANK), F32),
            vmem((len(CHIPS), 8, RANK), F32),
            vmem((8, RANK), F32),
            vmem((32, 8, RANK), F32),
            vmem((RANK, 2 * RANK), F32),
            vmem((HALF, RANK), F32),
            vmem((2, 2, 128, RANK), F32),
            vmem((2, 2, 2, 128, RANK), F32),
            vmem((2, 3, SMALL, RANK), F32),
            vmem((HALF, RANK), F32),
            vmem((8, RANK), F32),
            vmem((len(COLUMN), 8, RANK), F32),
            vmem((2, 8, RANK), F32),
            vmem((6, 8, RANK), F32),
            dma((4, 3)),
            dma((2,)),
            dma((2,)),
            dma((2,)),
            dma((2,)),
            dma((2,)),
            dma((2,)),
            dma((2, 2)),
            dma((3,)),
            dma((2,)),
            dma((2, 2)),
            dma((2, 2)),
            dma((5,)),
            dma((2, 2, 5)),
            dma((5, 2)),
            dma((2,)),
            dma((2,)),
            dma((1,)),
        ],
        compiler_params=pltpu.CompilerParams(
            collective_id=0, has_side_effects=True, vmem_limit_bytes=32 * 2**20
        ),
    )(mom, grad, fac, w)


def update_kernel(
    scal, w, b, right, basis, norm, new_w_out, new_mom_out, new_fac_out, new_w, new_mom, new_fac, sem
):
    decay, rate = scal[0], scal[1]
    s = norm[0:1, :]
    q = basis[...]
    scale = rate * jnp.sqrt(jnp.float32(4096 * 16384 / RANK))
    stacked = split(jnp.concatenate([q * (1.0 - decay), q * (s * scale)], axis=0))
    wide = 512
    for i in range(COLS // wide):
        at = pl.ds(i * wide, wide)
        r = right[at, :]
        new_fac[at, :] = r * s
        pltpu.make_async_copy(new_fac.at[at, :], new_fac_out.at[at, :], sem.at[2]).start()
        d = dot3(stacked, split(r), ((1,), (1,)))
        new_mom[:, at] = b[:, at] - d[:ROWS]
        pltpu.make_async_copy(new_mom.at[:, at], new_mom_out.at[:, at], sem.at[1]).start()
        new_w[:, at] = w[:, at] - d[ROWS:]
        pltpu.make_async_copy(new_w.at[:, at], new_w_out.at[:, at], sem.at[0]).start()
    pltpu.make_async_copy(new_w, new_w_out, sem.at[0]).wait()
    pltpu.make_async_copy(new_mom, new_mom_out, sem.at[1]).wait()
    pltpu.make_async_copy(new_fac, new_fac_out, sem.at[2]).wait()


def update_call(scal, w, b, right, basis, norm):
    here = pl.BlockSpec(memory_space=pltpu.VMEM)
    outs = [(ROWS, COLS), (ROWS, COLS), (COLS, RANK)]
    return pl.pallas_call(
        update_kernel,
        out_shape=[jax.ShapeDtypeStruct(shape, F32) for shape in outs],
        in_specs=[pl.BlockSpec(memory_space=pltpu.SMEM)] + [here] * 5,
        out_specs=[pl.BlockSpec(memory_space=pl.ANY)] * 3,
        scratch_shapes=[pltpu.VMEM(shape, F32) for shape in outs] + [pltpu.SemaphoreType.DMA((3,))],
        compiler_params=pltpu.CompilerParams(vmem_limit_bytes=24 * 2**20),
    )(scal, w, b, right, basis, norm)


def body(weight, momentum, gradient, factor, decay, rate):
    keep = [pltpu.with_memory_space_constraint(a, pltpu.HBM) for a in (momentum, gradient, factor, weight)]
    right, basis, norm, b, w = reduce_call(*keep)
    scal = jnp.stack([decay, rate])
    return tuple(update_call(scal, w, b, right, basis, norm))


def solution(mesh):
    placed = (P("fsdp", "tp"), P("fsdp", "tp"), P("fsdp", "tp"), P("tp", None), P(), P())
    return jax.shard_map(
        body,
        mesh=mesh,
        in_specs=placed,
        out_specs=(P("fsdp", "tp"), P("fsdp", "tp"), P("tp", None)),
        check_vma=False,
    )
```

```python
import jax
import jax.numpy as jnp
from jax import lax
from jax.experimental import pallas as pl
from jax.experimental.pallas import tpu as pltpu
from jax.sharding import PartitionSpec as P

F32 = jnp.float32
BF16 = jnp.bfloat16
HIGH = lax.Precision.HIGHEST
MESH = pl.DeviceIdType.MESH
NX = NY = NZ = 4
ROWS, COLS, RANK = 128, 4096, 256
HALF = COLS // 2
QUARTER = HALF // 2
BIG = QUARTER // 4
SMALL = BIG // 4
CHIPS = [(dx, dy) for dx in range(NX) for dy in range(NY) if dx or dy]
RING = (1, 3, 2)
ONWARD = {1: ((1, 0, 64), (2, 0, 32)), -1: ((3, 0, 64), (2, 32, 32))}
ROUNDS = (256, 384, 384, 128, 384)
COLUMN = [(dz, dc) for dz in range(NZ) for dc in range(2) if dz or dc]


def split(x):
    hi = x.astype(BF16)
    return hi, (x - hi.astype(F32)).astype(BF16)


def dot3(a, b, dims):
    (ah, al), (bh, bl) = a, b

    def one(p, q):
        return lax.dot_general(p, q, (dims, ((), ())), preferred_element_type=F32)

    if dims[0] == (1,):
        n = ah.shape[0]
        both = one(jnp.concatenate([ah, al], axis=0), bh)
        return both[:n] + (both[n:] + one(ah, bl))
    return one(ah, bh) + (one(ah, bl) + one(al, bh))


def dot6(a, b, dims):
    return lax.dot_general(a, b, (dims, ((), ())), precision=HIGH, preferred_element_type=F32)


def row_of(t, s):
    return jnp.broadcast_to(t[s : s + 1, :], (8, 128))


def lane_of(t, l):
    return jnp.broadcast_to(t[:, l : l + 1], (8, 128))


def eliminate(d, between=None):
    nb, nt = 64, 8
    lane = lax.broadcasted_iota(jnp.int32, (8, 128), 1)
    sub = lax.broadcasted_iota(jnp.int32, (8, 128), 0)
    w = []
    for i in range(nt):
        tile = jnp.concatenate([d[8 * i : 8 * i + 8, :], jnp.zeros((8, 128 - nb), F32)], axis=1)
        w.append(jnp.where(lane == nb + 8 * i + sub, 1.0, tile))
    out = []
    for k in range(nt):
        if k == nt // 2 and between is not None:
            between()
        tile = w[k]
        cs = [lane_of(tile, 8 * k + j) for j in range(8)]
        others = [[lane_of(w[i], 8 * k + j) for j in range(8)] for i in range(k + 1, nt)]
        v = tile
        for p in range(8):
            piv = row_of(cs[p], p)
            inv = 1.0 / piv
            row = row_of(tile, p)
            mine = sub == p
            v = jnp.where(mine, row * lax.rsqrt(piv), v)
            rn = row * inv
            cz = jnp.where(mine, 0.0, cs[p])
            tile = jnp.where(mine, rn, tile) - cz * rn
            for j in range(p + 1, 8):
                rj = row_of(cs[j], p) * inv
                cs[j] = jnp.where(mine, rj, cs[j]) - cz * rj
        out.append(v)
        if k + 1 < nt:
            ts = [row_of(tile, p) for p in range(8)]
            for i in range(k + 1, nt):
                acc = [others[i - k - 1][p] * ts[p] for p in range(8)]
                while len(acc) > 1:
                    acc = [acc[q] + acc[q + 1] for q in range(0, len(acc), 2)]
                w[i] = w[i] - acc[0]
    return jnp.concatenate([o[:, nb : 2 * nb] for o in out], axis=0)


def inverse_block(m, k, between=None):
    return eliminate(m[64 * k : 64 * k + 64, 64 * k : 64 * k + 64], between)


def factor_block(m, k, inv):
    lo, hi = 64 * k, 64 * k + 64
    v = dot6(inv, m[lo:hi, :], ((1,), (0,)))
    m[lo:hi, :] = v
    if hi < RANK:
        ut = v[:, :RANK].T[hi:, :]
        m[hi:, :] -= dot6(ut, v, ((1,), (0,)))


def reduce_kernel(
    mom_hbm, grad_hbm, fac_hbm, w_hbm, right, basis, norm, mom, w,
    grad, fac, peer_b, turned, zbuf, left, gsend, grecv, gown, gram, m, gp, fwd, rs1, rs2, raw, sq_own, sq_in, sq_sum, sq_end,
    load_sem, b_sem, z_sem, l_sem, g_sem, gg_sem, cg_sem, fwd_sem, rs1_send, rs1_sem, late_sem, own_sem, rs2_sem, ag1_sem, ag2_send, ag2_sem,
    core_sem, sq_sem, sqe_sem, w_sem,
):
    f = lax.axis_index("fsdp")
    z = lax.axis_index("tp")
    y, x, c = f // 8, (f // 2) % 4, f % 2

    def fence():
        @pl.when(z < 0)
        def _():
            gown[...] = gown[...] + 1.0

    def at(dx=0, dy=0, dc=0, dz=0):
        return ((((y + dy) % 4) * 4 + (x + dx) % 4) * 2 + (c + dc) % 2, (z + dz) % 4)

    def copy(src, dst, send_sem, recv_sem, where):
        return pltpu.make_async_remote_copy(
            src, dst, send_sem, recv_sem, device_id=where, device_id_type=MESH
        )

    drains = []

    def send(src, dst, send_sem, recv_sem, where):
        cp = copy(src, dst, send_sem, recv_sem, where)
        cp.start()
        return cp

    def group(ref, send_sem, recv_sem):
        return copy(ref, ref, send_sem, recv_sem, at(dc=1))

    def write(src, dst, sem):
        cp = pltpu.make_async_copy(src, dst, sem)
        cp.start()
        return cp

    def rows(start, size):
        return pl.ds(pl.multiple_of(start, size), size)

    fence()
    barrier = pltpu.get_barrier_semaphore()
    partners = [at(dx, dy) for dx, dy in CHIPS] + [at(dz=dz, dc=dc) for dz, dc in COLUMN]
    for partner in partners:
        pl.semaphore_signal(barrier, inc=1, device_id=partner, device_id_type=MESH)
    blocks, ahead = 4, 4
    wide = COLS // blocks

    def load(q):
        cols = pl.ds(q * wide, wide)
        trio = [
            pltpu.make_async_copy(mom_hbm.at[:, cols], mom.at[:, cols], load_sem.at[q, 0]),
            pltpu.make_async_copy(grad_hbm.at[:, cols], grad.at[:, cols], load_sem.at[q, 1]),
            pltpu.make_async_copy(fac_hbm.at[cols, :], fac.at[cols, :], load_sem.at[q, 2]),
        ]
        for cp in trio:
            cp.start()
        return trio

    loads = [load(q) for q in range(ahead)]

    fence()
    part = None
    for q in range(blocks):
        for cp in loads[q]:
            cp.wait()
        if q + ahead < blocks:
            loads.append(load(q + ahead))
        cols = pl.ds(q * wide, wide)
        b = mom[:, cols] + grad[:, cols].astype(F32)
        mom[:, cols] = b
        p = dot3(split(b), split(fac[cols, :]), ((1,), (0,)))
        part = p if part is None else part + p
    zbuf[z] = part
    fence()
    pl.semaphore_wait(barrier, len(partners))
    fence()
    for dz in RING:
        send(zbuf.at[z], zbuf.at[z], z_sem.at[0], z_sem.at[1], at(dz=dz))
    z_all = group(zbuf.at[0:3], z_sem.at[0], z_sem.at[1])
    b_cp = send(mom.at[:, rows((1 - c) * HALF, HALF)], peer_b, b_sem.at[0], b_sem.at[1], at(dc=1))
    drains += [z_all, b_cp]
    w_cp = write(w_hbm, w, w_sem.at[0])
    fence()
    b_cp.wait_recv()
    for i in range(HALF // BIG):
        part = jnp.concatenate([mom[:, rows(c * HALF + i * BIG, BIG)], peer_b[:, i * BIG : (i + 1) * BIG]], axis=0)
        hi, lo = split(part.T)
        turned[0, i * BIG : (i + 1) * BIG, :] = hi
        turned[1, i * BIG : (i + 1) * BIG, :] = lo
    fence()
    z_all.wait_recv()
    left[0] = (zbuf[0] + zbuf[1]) + (zbuf[2] + zbuf[3])
    l_cp = send(left.at[0], left.at[1], l_sem.at[0], l_sem.at[1], at(dc=1))
    drains.append(l_cp)
    fence()
    l_cp.wait_recv()
    both = left[...].reshape(2 * ROWS, RANK)

    fence()
    lh, ll = split(both)

    def product(start):
        place = rows(start, BIG)
        gp[place, :] = dot3((turned[0, place, :], turned[1, place, :]), (lh, ll), ((1,), (0,)))

    def step(h, d):
        return at(dx=d) if h == 0 else at(dy=d)

    def cross(h, d):
        return at(dy=d) if h == 0 else at(dx=d)

    along, across = (x, y), (y, x)
    both_h = (0, 1)

    def chunk(h, d):
        return h * QUARTER + ((along[h] + d) % 4) * BIG

    def sub(h, j, k, first=0):
        return chunk(h, j) + ((across[h] + k) % 4) * SMALL + first

    def onward(h, d, j, subs, buffer, send_sem, recv_sem):
        for k, first, size in subs:
            here = pl.ds(k * SMALL + first, size)
            send(gp.at[rows(sub(h, j, k, first), size), :], buffer.at[here, :], send_sem, recv_sem, step(h, d))

    def add(h, j, subs, buffer):
        for k, first, size in subs:
            place = rows(sub(h, j, k, first), size)
            gp[place, :] = gp[place, :] + buffer[k * SMALL + first : k * SMALL + first + size, :]

    def side(d):
        return (1 - d) // 2

    def late(d):
        return ((0, 16 - 16 * d, 32),)

    for h in both_h:
        far = chunk(h, 2)
        product(far)
        for d in (1, -1):
            onward(h, d, 2, ONWARD[d], fwd.at[h, side(d)], rs1_send.at[0], fwd_sem.at[h, side(d)])
    fence()
    mine = left[:, :, rows(c * 128, 128)].reshape(2 * ROWS, 128)
    gsend[...] = dot6(mine, both, ((0,), (0,)))
    fence()
    chip = y * 4 + x
    for i, (dx, dy) in enumerate(CHIPS):
        other = ((y + dy) % 4) * 4 + (x + dx) % 4
        send(gsend.at[rows(other * 8, 8), :], grecv.at[i], g_sem.at[0], g_sem.at[1], at(dx, dy))
    g_all = group(grecv, g_sem.at[0], g_sem.at[1])

    fence()
    for h in both_h:
        product(chunk(h, 1))
        product(chunk(h, -1))
    for h in both_h:
        product(chunk(h, 0))
    fence()
    for h in both_h:
        for d in (1, -1):
            onward(h, d, d, ONWARD[-d], rs1.at[h, side(d)], rs1_send.at[1], rs1_sem.at[h])
    for h in both_h:
        for d in (1, -1):
            onward(h, d, 2, late(d), fwd.at[h, side(d)], rs1_send.at[3], late_sem.at[h, side(d)])
    for n, size in ((0, 384), (3, 128), (4, 256)):
        drains.append(group(gp.at[0:size], rs1_send.at[n], fwd_sem.at[0, 0]))
    fence()
    for h in both_h:
        for d in (1, -1):
            group(gp.at[0:96], rs1_send.at[0], fwd_sem.at[h, side(d)]).wait_recv()
            add(h, d, ONWARD[d], fwd.at[h, side(d)])
            onward(h, d, d, ONWARD[d], rs1.at[h, side(d)], rs1_send.at[2], rs1_sem.at[h])
    fence()
    g_all.wait_recv()
    total = gsend[rows(chip * 8, 8), :]
    for i in range(len(CHIPS)):
        total = total + grecv[i]
    fence()
    gown[...] = total
    gram[c * 16 + chip] = total
    for dx, dy in CHIPS:
        send(gown, gram.at[c * 16 + chip], gg_sem.at[0], gg_sem.at[1], at(dx, dy))
    gg_all = group(grecv, gg_sem.at[0], gg_sem.at[1])
    drains += [g_all, gg_all]

    fence()
    for h in both_h:
        for d in (1, -1):
            group(gp.at[0:32], rs1_send.at[3], late_sem.at[h, side(d)]).wait_recv()
            add(h, d, late(d), fwd.at[h, side(d)])
            onward(h, d, d, ((0, 0, SMALL),), rs1.at[h, side(d)], rs1_send.at[4], own_sem.at[h])
    fence()
    for h in both_h:
        rs1_all = group(gp.at[0:384], rs1_send.at[1 + h], rs1_sem.at[h])
        drains.append(rs1_all)
        rs1_all.wait_recv()
        for i, d in enumerate((2, 1, 3)):
            for n in (0, 1):
                add(h, 0, ((d, 0, SMALL),), rs1.at[h, n])
            place = rows(sub(h, 0, d), SMALL)
            send(gp.at[place, :], rs2.at[h, i], rs2_sem.at[h, 0], rs2_sem.at[h, 1], cross(h, d))
    fence()
    gg_all.wait_recv()
    half_gram = gram.at[pl.ds(c * 16, 16)]
    core_gram = send(half_gram, half_gram, cg_sem.at[0], cg_sem.at[1], at(dc=1))
    drains.append(core_gram)
    r_id = lax.broadcasted_iota(jnp.int32, (RANK, RANK), 0)
    c_id = lax.broadcasted_iota(jnp.int32, (RANK, RANK), 1)
    m[:, RANK:] = jnp.where(r_id == c_id, 1.0, 0.0).astype(F32)
    fence()
    core_gram.wait_recv()
    m[:, :RANK] = gram[...].reshape(RANK, RANK)
    fence()
    inv0 = inverse_block(m, 0)
    fence()
    ag1_all = []
    for h in both_h:
        rs2_all = group(rs2.at[h], rs2_sem.at[h, 0], rs2_sem.at[h, 1])
        rs2_all.wait_recv()
        group(gp.at[0:128], rs1_send.at[4], own_sem.at[h]).wait_recv()
        for n in (0, 1):
            add(h, 0, ((0, 0, SMALL),), rs1.at[h, n])
        place = rows(chunk(h, 0) + across[h] * SMALL, SMALL)
        raw[place, :] = (gp[place, :] + rs2[h, 0]) + (rs2[h, 1] + rs2[h, 2])
        for d in (2, 1, 3):
            send(raw.at[place, :], raw.at[place, :], ag1_sem.at[h, 0], ag1_sem.at[h, 1], cross(h, d))
        ag1_all.append(group(rs2.at[h], ag1_sem.at[h, 0], ag1_sem.at[h, 1]))
        drains += [rs2_all, ag1_all[h]]
    fence()
    factor_block(m, 0, inv0)
    fence()
    inv1 = inverse_block(m, 1)
    fence()
    def gather(n, h, d, j, subs):
        for k, first, size in subs:
            start = chunk(h, j) + ((across[h] + k) % 4) * SMALL + first
            piece = raw.at[rows(start, size), :]
            send(piece, piece, ag2_send.at[n], ag2_sem.at[h, (1 - d) // 2, n], step(h, d))

    def gathered(n, h, d):
        size = ROUNDS[n] // 4
        group(raw.at[0:size], ag2_send.at[n], ag2_sem.at[h, (1 - d) // 2, n]).wait_recv()

    for h in both_h:
        for d in (1, -1):
            gather(0, h, d, 0, ((0, 0, SMALL),))
    fence()
    factor_block(m, 1, inv1)
    def first_round():
        fence()
        for cp in ag1_all:
            cp.wait_recv()
        for h in both_h:
            for d in (1, -1):
                gather(1, h, d, 0, ONWARD[d])
        fence()

    def second_round():
        fence()
        for h in both_h:
            for d in (1, -1):
                gather(2, h, d, 0, ONWARD[-d])
        for h in both_h:
            for d in (1, -1):
                gathered(0, h, d)
                gather(3, h, d, -d, ((0, 16 - 16 * d, 32),))
        fence()

    fence()
    inv2 = inverse_block(m, 2, first_round)
    fence()
    factor_block(m, 2, inv2)
    fence()
    inv3 = inverse_block(m, 3, second_round)
    fence()
    factor_block(m, 3, inv3)

    fence()
    upper = m[:, RANK:].T
    inv = split(upper)
    groups = [
        [(chunk(h, 0), BIG) for h in both_h],
        [(chunk(h, -1), BIG) for h in both_h],
        [(chunk(h, 1), BIG) for h in both_h],
        [(chunk(0, 2), BIG)],
        [(chunk(1, 2), BIG)],
    ]

    def finish(g):
        pieces = jnp.concatenate([raw[rows(start, size), :] for start, size in groups[g]], axis=0)
        r = dot3(split(pieces), inv, ((1,), (0,)))
        done = 0
        for start, size in groups[g]:
            mine = rows(c * HALF + start, size)
            right[mine, :] = r[done : done + size]
            send(right.at[mine, :], right.at[mine, :], core_sem.at[g, 0], core_sem.at[g, 1], at(dc=1))
            done += size
        return r

    own = finish(0)
    for h in both_h:
        part = own[h * BIG : (h + 1) * BIG]
        sq_own[h : h + 1, :] = jnp.sum(part * part, axis=0, keepdims=True)
    for i, (dz, dc) in enumerate(COLUMN):
        send(sq_own.at[0:2], sq_in.at[i, 0:2], sq_sem.at[0], sq_sem.at[1], at(dz=dz, dc=dc))
    sq_all = group(sq_in.at[:, 0:2], sq_sem.at[0], sq_sem.at[1])
    drains.append(sq_all)
    fence()
    for h in both_h:
        for d in (1, -1):
            gathered(1, h, d)
            gather(4, h, d, -d, ONWARD[d])
    drains += [group(raw.at[0:size], ag2_send.at[n], ag2_sem.at[0, 0, n]) for n, size in enumerate(ROUNDS)]
    fence()
    basis[...] = dot6(left[0], upper, ((1,), (0,)))
    fence()
    for h in both_h:
        gathered(2, h, 1)
        gathered(2, h, -1)
    fence()
    finish(1)
    finish(2)
    fence()
    sq_all.wait_recv()
    total = sq_own[0:2, :]
    for i in range(len(COLUMN)):
        total = total + sq_in[i, 0:2, :]
    fence()
    for h in both_h:
        sq_sum[h, 0:1, :] = total[h : h + 1, :]
        for i, d in enumerate((2, 1, 3)):
            send(sq_sum.at[h, 0:1], sq_end.at[h * 3 + i, 0:1], sqe_sem.at[0], sqe_sem.at[1], step(h, d))
    sqe_all = group(sq_end.at[:, 0:1], sqe_sem.at[0], sqe_sem.at[1])
    drains.append(sqe_all)
    fence()
    for h in both_h:
        for d in (1, -1):
            gathered(3, h, d)
            gathered(4, h, d)
        fence()
        finish(3 + h)
        fence()
    for g, pieces in enumerate(groups):
        core_all = group(right.at[0 : sum(size for _, size in pieces)], core_sem.at[g, 0], core_sem.at[g, 1])
        drains.append(core_all)
        core_all.wait_recv()
    fence()
    sqe_all.wait_recv()
    total = sq_sum[0, 0:1, :] + sq_sum[1, 0:1, :]
    for i in range(6):
        total = total + sq_end[i, 0:1, :]
    norm[...] = jnp.broadcast_to(lax.rsqrt(total + 1e-06), (8, RANK))
    fence()
    for cp in drains:
        cp.wait_send()
    w_cp.wait()


def reduce_call(mom, grad, fac, w):
    vmem = pltpu.VMEM
    dma = pltpu.SemaphoreType.DMA
    return pl.pallas_call(
        reduce_kernel,
        out_shape=(
            jax.ShapeDtypeStruct((COLS, RANK), F32),
            jax.ShapeDtypeStruct((ROWS, RANK), F32),
            jax.ShapeDtypeStruct((8, RANK), F32),
            jax.ShapeDtypeStruct((ROWS, COLS), F32),
            jax.ShapeDtypeStruct((ROWS, COLS), F32),
        ),
        in_specs=[pl.BlockSpec(memory_space=pltpu.HBM)] * 4,
        out_specs=[pl.BlockSpec(memory_space=vmem)] * 5,
        scratch_shapes=[
            vmem((ROWS, COLS), BF16),
            vmem((COLS, RANK), F32),
            vmem((ROWS, HALF), F32),
            vmem((2, HALF, RANK), BF16),
            vmem((NZ, ROWS, RANK), F32),
            vmem((2, ROWS, RANK), F32),
            vmem((128, RANK), F32),
            vmem((len(CHIPS), 8, RANK), F32),
            vmem((8, RANK), F32),
            vmem((32, 8, RANK), F32),
            vmem((RANK, 2 * RANK), F32),
            vmem((HALF, RANK), F32),
            vmem((2, 2, BIG, RANK), F32),
            vmem((2, 2, BIG, RANK), F32),
            vmem((2, 3, SMALL, RANK), F32),
            vmem((HALF, RANK), F32),
            vmem((8, RANK), F32),
            vmem((len(COLUMN), 8, RANK), F32),
            vmem((2, 8, RANK), F32),
            vmem((6, 8, RANK), F32),
            dma((4, 3)),
            dma((2,)),
            dma((2,)),
            dma((2,)),
            dma((2,)),
            dma((2,)),
            dma((2,)),
            dma((2, 2)),
            dma((5,)),
            dma((2,)),
            dma((2, 2)),
            dma((2,)),
            dma((2, 2)),
            dma((2, 2)),
            dma((5,)),
            dma((2, 2, 5)),
            dma((5, 2)),
            dma((2,)),
            dma((2,)),
            dma((1,)),
        ],
        compiler_params=pltpu.CompilerParams(
            collective_id=0, has_side_effects=True, vmem_limit_bytes=32 * 2**20
        ),
    )(mom, grad, fac, w)


def update_kernel(
    scal, w, b, right, basis, norm, new_w_out, new_mom_out, new_fac_out, new_w, new_mom, new_fac, sem
):
    decay, rate = scal[0], scal[1]
    s = norm[0:1, :]
    q = basis[...]
    scale = rate * jnp.sqrt(jnp.float32(4096 * 16384 / RANK))
    stacked = split(jnp.concatenate([q * (1.0 - decay), q * (s * scale)], axis=0))
    wide = 512
    for i in range(COLS // wide):
        at = pl.ds(i * wide, wide)
        r = right[at, :]
        new_fac[at, :] = r * s
        pltpu.make_async_copy(new_fac.at[at, :], new_fac_out.at[at, :], sem.at[2]).start()
        d = dot3(stacked, split(r), ((1,), (1,)))
        new_mom[:, at] = b[:, at] - d[:ROWS]
        pltpu.make_async_copy(new_mom.at[:, at], new_mom_out.at[:, at], sem.at[1]).start()
        new_w[:, at] = w[:, at] - d[ROWS:]
        pltpu.make_async_copy(new_w.at[:, at], new_w_out.at[:, at], sem.at[0]).start()
    pltpu.make_async_copy(new_w, new_w_out, sem.at[0]).wait()
    pltpu.make_async_copy(new_mom, new_mom_out, sem.at[1]).wait()
    pltpu.make_async_copy(new_fac, new_fac_out, sem.at[2]).wait()


def update_call(scal, w, b, right, basis, norm):
    here = pl.BlockSpec(memory_space=pltpu.VMEM)
    outs = [(ROWS, COLS), (ROWS, COLS), (COLS, RANK)]
    return pl.pallas_call(
        update_kernel,
        out_shape=[jax.ShapeDtypeStruct(shape, F32) for shape in outs],
        in_specs=[pl.BlockSpec(memory_space=pltpu.SMEM)] + [here] * 5,
        out_specs=[pl.BlockSpec(memory_space=pl.ANY)] * 3,
        scratch_shapes=[pltpu.VMEM(shape, F32) for shape in outs] + [pltpu.SemaphoreType.DMA((3,))],
        compiler_params=pltpu.CompilerParams(vmem_limit_bytes=24 * 2**20),
    )(scal, w, b, right, basis, norm)


def body(weight, momentum, gradient, factor, decay, rate):
    keep = [pltpu.with_memory_space_constraint(a, pltpu.HBM) for a in (momentum, gradient, factor, weight)]
    right, basis, norm, b, w = reduce_call(*keep)
    scal = jnp.stack([decay, rate])
    return tuple(update_call(scal, w, b, right, basis, norm))


def solution(mesh):
    placed = (P("fsdp", "tp"), P("fsdp", "tp"), P("fsdp", "tp"), P("tp", None), P(), P())
    return jax.shard_map(
        body,
        mesh=mesh,
        in_specs=placed,
        out_specs=(P("fsdp", "tp"), P("fsdp", "tp"), P("tp", None)),
        check_vma=False,
    )
```
